32 devices in a mesh: seq: 4 (over x, core), ctx: 8 (over z, y).
Axes of the slice: x: 2, y: 2, z: 4, core: 2. Of those that a mesh axis runs over, the one named last changes fastest.
Arguments:
- tokens: bfloat16 [3, 4, 768, 767], P(None, 'seq', 'ctx'), may hold values from -6 to 6
- segment_ids: int32 [3, 4, 768], P(None, 'seq'), may hold values from 0 to 7, never falling along the last dimension, each value on 1 to 576 neighbouring positions
- qkv_weight: bfloat16 [768, 2304], P(('seq', 'ctx')), may hold values from -0.21875 to 0.21875
- out_weight: bfloat16 [768, 767], P(('seq', 'ctx')), may hold values from -0.875 to 0.875
- up_weight: bfloat16 [768, 3072], P(('seq', 'ctx')), may hold values from -0.21875 to 0.21875
- down_weight: bfloat16 [3072, 767], P(('seq', 'ctx')), may hold values from -0.109375 to 0.109375
- attn_gain: bfloat16 [768], P(('seq', 'ctx')), may hold values from 0.099609375 to 1.8984375
- mlp_gain: bfloat16 [768], P(('seq', 'ctx')), may hold values from 0.099609375 to 1.8984375
- out_cotangent: bfloat16 [3, 4, 768, 767], P(None, 'seq', 'ctx'), may hold values from -6 to 6
Outputs:
- result: float32 [3, 4, 768, 767], P(None, 'seq', 'ctx')
- grad_tokens: float32 [3, 4, 768, 767], P(None, 'seq', 'ctx')
- grad_qkv_weight: float32 [768, 2304], P(('seq', 'ctx'))
- grad_out_weight: float32 [768, 767], P(('seq', 'ctx'))
- grad_up_weight: float32 [768, 3072], P(('seq', 'ctx'))
- grad_down_weight: float32 [3072, 767], P(('seq', 'ctx'))
- grad_attn_gain: float32 [768], P(('seq', 'ctx'))
- grad_mlp_gain: float32 [768], P(('seq', 'ctx'))
The draws below stay inside these ranges and needn't reach their ends.
Inputs may be any that keep to these rules, and one draw needn't show every extreme that they name: `segment_ids`: along each sequence the ids never fall; each of the 8 documents of a sequence has 1 to 576 tokens, and one has exactly 576.
All inputs are finite; a program needn't handle non-finite values.
Results may differ from the reference program's by a relative error of at most 0.014.
Values may be sent and summed in bfloat16 or wider, within the bound.
No kernel may reach another device: no remote copies, remote signals or barrier semaphores. Data moves between devices by JAX's collectives and lax.ppermute only.
A program may use at most 384 MiB of HBM per device.

```python
import math
import jax
import jax.numpy as jnp
import numpy as np
from jax import lax

D = 768
HEADS = 12
HEAD_DIM = 64
FF = 3072
RES = 767
SEQ_LEN = 768
SEQ_ALL = 4
MICRO = 3
DOCS = 8
DOC_MOST = 576


def draw_tokens(key, part):
    key = jax.random.fold_in(key, 11)
    rough_key, line_key, sign_key = jax.random.split(key, 3)
    shape = (MICRO, SEQ_ALL, SEQ_LEN, RES)
    rough = jax.random.normal(rough_key, shape, jnp.float32)
    direction = jax.random.normal(line_key, (MICRO, SEQ_ALL, 1, RES), jnp.float32)
    flips = jnp.where(jax.random.bernoulli(sign_key, 0.5, (MICRO, SEQ_ALL, 1, 1)), 1.0, -1.0)
    places = jnp.arange(SEQ_LEN, dtype=jnp.float32)
    ramp = (2.0 * places / (SEQ_LEN - 1) - 1.0)[None, None, :, None]
    values = rough + 1.25 * flips * ramp * direction
    return jnp.clip(values, -6.0, 6.0).astype(jnp.bfloat16)


def levels(stream_key, shape, pieces, smallest, top_value):
    loudness, own = 1.0, jax.random.fold_in(stream_key, 6)
    for axis_at, parts in pieces:
        heights = jnp.exp(jax.random.uniform(jax.random.fold_in(own, axis_at), (parts,), jnp.float32, smallest / len(pieces), top_value / len(pieces)))
        loudness = loudness * jnp.repeat(heights, shape[axis_at] // parts).reshape([-1 if axis == axis_at else 1 for axis in range(len(shape))])
    return loudness


def split_up(amount, total, bound, skew):
    portions = [(1 << 20) // math.isqrt(grade ** skew) + 1 for grade in range(2, amount + 1)]
    spare, given = total - bound - (amount - 1), [1] * (amount - 1)
    while spare > 0:
        candidates = [i for i in range(amount - 1) if given[i] < bound]
        whole, budget = sum([portions[i] for i in candidates]), spare
        for i in candidates:
            extra = min(bound - given[i], max(1, budget * portions[i] // whole), spare)
            given[i] = given[i] + extra
            spare = spare - extra
    return np.array([bound] + given)


def uneven_parts(rng, count, total, most, lean):
    if count == 2:
        one = jax.random.randint(rng, (), max(1, total - most), min(most, total - 1) + 1)
        return jnp.stack([one, total - one])
    sizes = jnp.asarray(split_up(count, total, most, lean), jnp.int32)
    couples = (count - 1) // 2
    donor, taker = sizes[1:1 + 2 * couples:2], sizes[2:2 + 2 * couples:2]
    slack = jnp.minimum(donor - 1, most - taker)
    passed = jax.random.randint(jax.random.fold_in(rng, 1), (couples,), 0, 1 << 20) % (slack + 1)
    sizes = sizes.at[1:1 + 2 * couples:2].set(donor - passed).at[2:2 + 2 * couples:2].set(taker + passed)
    return sizes[jax.random.permutation(jax.random.fold_in(rng, 2), count)]


def gaussian(own_key, shape, deviation, reach, pieces=(), kind=jnp.bfloat16):
    level = levels(own_key, shape, pieces, -0.22, 0.18) if pieces else 1.0
    array = jax.random.normal(own_key, shape, jnp.float32) * deviation * level
    return jnp.minimum(jnp.maximum(array, -reach), reach).astype(kind)


def setup_inputs(seed: int = 0) -> dict:
    streams_of = jax.random.split(jax.random.key(seed), 10)
    return {
        "tokens": draw_tokens(jax.random.fold_in(streams_of[9], 71), 0),
        "segment_ids": jax.vmap(lambda own: jnp.searchsorted(jnp.cumsum(uneven_parts(own, DOCS, SEQ_LEN, DOC_MOST, 2)), jnp.arange(SEQ_LEN), side="right"))(jax.random.split(streams_of[1], MICRO * SEQ_ALL)).reshape((MICRO, SEQ_ALL, SEQ_LEN)).astype(jnp.int32),
        "qkv_weight": gaussian(streams_of[2], (D, 3 * D), D ** -0.5, 0.21875, ((0, 32),)),
        "out_weight": gaussian(streams_of[3], (D, RES), (D // 16) ** -0.5, 0.875, ((0, 32),)),
        "up_weight": gaussian(streams_of[4], (D, FF), D ** -0.5, 0.21875, ((0, 32),)),
        "down_weight": gaussian(streams_of[5], (FF, RES), FF ** -0.5, 0.109375, ((0, 32),)),
        "attn_gain": jnp.clip(1.0 + 0.18 * jax.random.normal(streams_of[6], (D,), jnp.float32), 0.099609375, 1.8984375).astype(jnp.bfloat16),
        "mlp_gain": jnp.clip(1.0 + 0.18 * jax.random.normal(streams_of[7], (D,), jnp.float32), 0.099609375, 1.8984375).astype(jnp.bfloat16),
        "out_cotangent": gaussian(streams_of[8], (MICRO, SEQ_ALL, SEQ_LEN, RES), 1.0, 6.0, ((1, 4), (2, 8))),
    }


EPS = 1e-05
NEG = -1e+30
SCALE = 0.125
HIGH = lax.Precision.HIGHEST

@jax.custom_vjp
def low(v):
    return lax.optimization_barrier(v.astype(jnp.bfloat16)).astype(jnp.float32)

@jax.custom_vjp
def low_back(v):
    return v

def low_keep(v):
    return (low(v), None)

def low_pass(kept, grad):
    return (grad,)

def back_keep(v):
    return (v, None)

def back_low(kept, grad):
    return (low(grad),)
low.defvjp(low_keep, low_pass)
low_back.defvjp(back_keep, back_low)

def matmul(left, right):
    return jnp.dot(left, right, precision=HIGH, preferred_element_type=jnp.float32)

def crms(inputs, gains):
    totals = lax.optimization_barrier(jnp.sum(inputs, axis=-1, keepdims=True))
    meansq = (lax.optimization_barrier(jnp.sum(inputs * inputs, axis=-1, keepdims=True)) + totals * totals) / gains.shape[0]
    return jnp.concatenate([inputs, -totals], axis=-1) * lax.rsqrt(meansq + EPS) * gains

def one_sequence(inputs, segments, qkv_weight, out_weight, up_weight, down_weight, attn_gain, mlp_gain):
    length = inputs.shape[0]
    width = qkv_weight.shape[0]
    norm_a = low(crms(inputs, attn_gain))
    qkv = low(low_back(matmul(norm_a, qkv_weight)))
    queries = qkv[:, :width].reshape(length, HEADS, HEAD_DIM)
    keys_all = qkv[:, width:2 * width].reshape(length, HEADS, HEAD_DIM)
    values_all = qkv[:, 2 * width:].reshape(length, HEADS, HEAD_DIM)
    block_len = math.gcd(length, 512)
    places = jnp.arange(length, dtype=jnp.int32)

    def attend(number):
        begin = (number * block_len).astype(jnp.int32)
        query_part = lax.dynamic_slice_in_dim(queries, begin, block_len, 0)
        seg_part = lax.dynamic_slice_in_dim(segments, begin, block_len, 0)
        place_part = begin + jnp.arange(block_len, dtype=jnp.int32)
        scores = jnp.einsum('qhd,khd->hqk', query_part, keys_all, precision=HIGH) * SCALE
        scores = low_back(scores)
        allowed = (seg_part[:, None] == segments[None, :]) & (place_part[:, None] >= places[None, :])
        probs = jax.nn.softmax(jnp.where(allowed[None], scores, NEG), axis=-1)
        return jnp.einsum('hqk,khd->qhd', low(probs), values_all, precision=HIGH)
    heads_out = lax.map(jax.checkpoint(attend), jnp.arange(length // block_len, dtype=jnp.int32))
    attn = low(low_back(heads_out.reshape(length, width)))
    mixed = inputs + low_back(matmul(attn, out_weight))
    norm_m = low(crms(mixed, mlp_gain))
    pre = low_back(matmul(norm_m, up_weight))
    act = low(jax.nn.gelu(pre, approximate=True))
    return mixed + low_back(matmul(act, down_weight))

def reference(tokens, segment_ids, qkv_weight, out_weight, up_weight, down_weight, attn_gain, mlp_gain, out_cotangent):
    inputs = tokens.astype(jnp.float32).reshape(-1, SEQ_LEN, RES)
    segments = segment_ids.reshape(-1, SEQ_LEN)
    params = tuple((matrix.astype(jnp.float32) for matrix in (qkv_weight, out_weight, up_weight, down_weight, attn_gain, mlp_gain)))

    def whole(rows_in, *weights):

        def advance(carry, pair):
            return (carry, one_sequence(pair[0], pair[1], *weights))
        _, outputs = lax.scan(advance, None, (rows_in, segments))
        return outputs
    outputs, pull = jax.vjp(whole, inputs, *params)
    grads = pull(out_cotangent.astype(jnp.float32).reshape(outputs.shape))
    return (outputs.reshape(tokens.shape), grads[0].reshape(tokens.shape), grads[1], grads[2], grads[3], grads[4], grads[5], grads[6])
```

```python
import math

import jax
import jax.numpy as jnp
import numpy as np
from jax import lax
from jax.experimental import pallas as pl
from jax.experimental.pallas import tpu as pltpu
from jax.sharding import PartitionSpec as P

HEADS = 12
HEAD_DIM = 64


EPS = 1e-05
NEG = -1e30
SCALE = 0.125


def crms(inputs, gains):
    totals = jnp.sum(inputs, axis=-1, keepdims=True)
    meansq = (jnp.sum(inputs * inputs, axis=-1, keepdims=True) + totals * totals) / gains.shape[0]
    return jnp.concatenate([inputs, -totals], axis=-1) * lax.rsqrt(meansq + EPS) * gains


def gelu_tanh(inputs):
    return jax.nn.gelu(inputs, approximate=True)


def matmul(left, right):
    return jnp.dot(left, right, preferred_element_type=jnp.float32)


def matmul_left_t(left, right):
    return lax.dot_general(
        left, right, (((0,), (0,)), ((), ())), preferred_element_type=jnp.float32
    )


def matmul_right_t(left, right):
    return lax.dot_general(
        left, right, (((1,), (1,)), ((), ())), preferred_element_type=jnp.float32
    )


def allowed_pairs(query_pos, query_seg, key_pos, key_seg):
    same_doc = query_seg[:, None, :, None] == key_seg[:, None, None, :]
    causal = query_pos[None, None, :, None] >= key_pos[None, None, None, :]
    return same_doc & causal


def attend_block(state, queries, query_pos, query_seg, keys, values, key_pos, key_seg):
    best, denom, accum = state
    scores = (
        jnp.einsum("bqhd,bkhd->bhqk", queries, keys, preferred_element_type=jnp.float32) * SCALE
    )
    allowed = allowed_pairs(query_pos, query_seg, key_pos, key_seg)
    scores = jnp.where(allowed, scores, NEG)
    peak = jnp.maximum(best, jnp.max(scores, axis=-1))
    weights = jnp.where(allowed, jnp.exp(scores - peak[..., None]), 0.0)
    factor = jnp.exp(best - peak)
    denom = denom * factor + jnp.sum(weights, axis=-1)
    accum = accum * factor[..., None] + jnp.einsum(
        "bhqk,bkhd->bhqd", weights.astype(jnp.bfloat16), values, preferred_element_type=jnp.float32
    )
    return (peak, denom, accum)


def pair_grads(queries, grad_o, lse, delta, query_pos, query_seg, keys, values, key_pos, key_seg):
    scores = (
        jnp.einsum("bqhd,bkhd->bhqk", queries, keys, preferred_element_type=jnp.float32) * SCALE
    )
    allowed = allowed_pairs(query_pos, query_seg, key_pos, key_seg)
    probs = jnp.where(allowed, jnp.exp(scores - lse[..., None]), 0.0)
    dprobs = jnp.einsum("bqhd,bkhd->bhqk", grad_o, values, preferred_element_type=jnp.float32)
    grad_scores = (probs * (dprobs - delta[..., None])).astype(jnp.bfloat16)
    part_q = (
        jnp.einsum("bhqk,bkhd->bqhd", grad_scores, keys, preferred_element_type=jnp.float32) * SCALE
    )
    part_k = (
        jnp.einsum("bhqk,bqhd->bkhd", grad_scores, queries, preferred_element_type=jnp.float32)
        * SCALE
    )
    part_v = jnp.einsum(
        "bhqk,bqhd->bkhd", probs.astype(jnp.bfloat16), grad_o, preferred_element_type=jnp.float32
    )
    return (part_q, part_k, part_v)


def body(
    tokens,
    segment_ids,
    qkv_weight,
    out_weight,
    up_weight,
    down_weight,
    attn_gain,
    mlp_gain,
    out_cotangent,
):
    micro_count, seq_count, local_len, res_width = tokens.shape
    length = segment_ids.shape[2]
    first = lax.axis_index("ctx") * local_len
    query_pos = first + jnp.arange(local_len, dtype=jnp.int32)
    row_count = seq_count * local_len

    def fetch():
        return (
            lax.all_gather(qkv_weight, ("seq", "ctx"), axis=0, tiled=True),
            lax.all_gather(out_weight, ("seq", "ctx"), axis=0, tiled=True),
            lax.all_gather(up_weight, ("seq", "ctx"), axis=0, tiled=True),
            lax.all_gather(down_weight, ("seq", "ctx"), axis=0, tiled=True),
            lax.all_gather(attn_gain, ("seq", "ctx"), axis=0, tiled=True),
            lax.all_gather(mlp_gain, ("seq", "ctx"), axis=0, tiled=True),
        )

    def backward(number, gathered, saved):
        qkv_full, out_full, up_full, down_full, gain_one, gain_two = gathered
        (
            inputs,
            seg_rows,
            query_seg,
            norm_a,
            queries,
            keys_own,
            values_own,
            attn_f32,
            lse,
            attn,
            mixed,
            norm_m,
            pre,
            act,
        ) = saved
        width = qkv_full.shape[0]
        grad_y = out_cotangent[number].reshape(row_count, res_width)
        grad_down = matmul_left_t(act, grad_y)
        grad_act = matmul_right_t(grad_y, down_full)
        _, gelu_pull = jax.vjp(gelu_tanh, pre)
        grad_pre = gelu_pull(grad_act)[0].astype(jnp.bfloat16)
        grad_up = matmul_left_t(norm_m, grad_pre)
        grad_norm_m = matmul_right_t(grad_pre, up_full)
        _, pull_two = jax.vjp(crms, mixed, gain_two.astype(jnp.float32))
        grad_mixed_norm, grad_gain_two = pull_two(grad_norm_m)
        grad_mixed = grad_y.astype(jnp.float32) + grad_mixed_norm
        grad_branch = grad_mixed.astype(jnp.bfloat16)
        grad_outw = matmul_left_t(attn, grad_branch)
        grad_attn = (
            matmul_right_t(grad_branch, out_full)
            .astype(jnp.bfloat16)
            .reshape(seq_count, local_len, HEADS, HEAD_DIM)
        )
        delta = jnp.transpose(jnp.sum(grad_attn.astype(jnp.float32) * attn_f32, axis=-1), (0, 2, 1))
        block_len = math.gcd(length, 1024)
        block_ids = jnp.arange(length // block_len, dtype=jnp.int32)
        keys_all, values_all = (
            lax.all_gather(keys_own, "ctx", axis=1, tiled=True),
            lax.all_gather(values_own, "ctx", axis=1, tiled=True),
        )

        def back_keys(carry, number_block):
            offset = number_block * block_len
            key_block = lax.dynamic_slice_in_dim(keys_all, offset, block_len, 1)
            value_block = lax.dynamic_slice_in_dim(values_all, offset, block_len, 1)
            key_pos = offset + jnp.arange(block_len, dtype=jnp.int32)
            key_seg = lax.dynamic_slice_in_dim(seg_rows, offset, block_len, 1)
            part_q, part_k, part_v = pair_grads(
                queries,
                grad_attn,
                lse,
                delta,
                query_pos,
                query_seg,
                key_block,
                value_block,
                key_pos,
                key_seg,
            )
            return (carry + part_q, jnp.concatenate([part_k, part_v], axis=-1))

        grad_q, terms = lax.scan(back_keys, jnp.zeros(queries.shape, jnp.float32), block_ids)
        terms = jnp.moveaxis(terms, 0, 1).reshape(seq_count, length, HEADS, 2 * HEAD_DIM)
        owned_terms = lax.psum_scatter(terms, "ctx", scatter_dimension=1, tiled=True)
        grad_k = owned_terms[..., :HEAD_DIM]
        grad_v = owned_terms[..., HEAD_DIM:]
        grad_qkv = jnp.concatenate(
            [
                grad_q.reshape(row_count, width),
                grad_k.reshape(row_count, width),
                grad_v.reshape(row_count, width),
            ],
            axis=-1,
        ).astype(jnp.bfloat16)
        grad_qkvw = matmul_left_t(norm_a, grad_qkv)
        grad_norm_a = matmul_right_t(grad_qkv, qkv_full)
        _, pull_one = jax.vjp(crms, inputs, gain_one.astype(jnp.float32))
        grad_input_norm, grad_gain_one = pull_one(grad_norm_a)
        grad_inputs = (grad_mixed + grad_input_norm).reshape(seq_count, local_len, res_width)
        return (
            grad_inputs,
            (grad_qkvw, grad_outw, grad_up, grad_down, grad_gain_one, grad_gain_two),
        )

    outputs = []
    input_grads = []
    owned = None
    for number in range(micro_count):
        (
            forward_qkv_full,
            forward_out_full,
            forward_up_full,
            forward_down_full,
            forward_gain_one,
            forward_gain_two,
        ) = fetch()
        forward_width = forward_qkv_full.shape[0]
        forward_inputs = tokens[number].astype(jnp.float32).reshape(row_count, res_width)
        forward_seg_rows = segment_ids[number]
        forward_query_seg = lax.dynamic_slice_in_dim(forward_seg_rows, first, local_len, 1)
        forward_norm_a = crms(forward_inputs, forward_gain_one.astype(jnp.float32)).astype(
            jnp.bfloat16
        )
        qkv = matmul(forward_norm_a, forward_qkv_full).astype(jnp.bfloat16)
        forward_queries = qkv[:, :forward_width].reshape(seq_count, local_len, HEADS, HEAD_DIM)
        forward_keys_own = qkv[:, forward_width : 2 * forward_width].reshape(
            seq_count, local_len, HEADS, HEAD_DIM
        )
        forward_values_own = qkv[:, 2 * forward_width :].reshape(
            seq_count, local_len, HEADS, HEAD_DIM
        )

        def fold_keys(state, piece):
            keys_part, values_part = piece
            span = keys_part.shape[1]
            block_len = span if span <= 1024 else math.gcd(span, 1024)

            def inner(carry, number_block):
                offset = number_block * block_len
                key_block = lax.dynamic_slice_in_dim(keys_part, offset, block_len, 1)
                value_block = lax.dynamic_slice_in_dim(values_part, offset, block_len, 1)
                key_pos = offset + jnp.arange(block_len, dtype=jnp.int32)
                key_seg = lax.dynamic_slice_in_dim(forward_seg_rows, offset, block_len, 1)
                return (
                    attend_block(
                        carry,
                        forward_queries,
                        query_pos,
                        forward_query_seg,
                        key_block,
                        value_block,
                        key_pos,
                        key_seg,
                    ),
                    None,
                )

            state, _ = lax.scan(inner, state, jnp.arange(span // block_len, dtype=jnp.int32))
            return state

        initial = (
            jnp.full((seq_count, HEADS, local_len), NEG, jnp.float32),
            jnp.zeros((seq_count, HEADS, local_len), jnp.float32),
            jnp.zeros((seq_count, HEADS, local_len, HEAD_DIM), jnp.float32),
        )
        best, denom, accum = fold_keys(
            initial,
            (
                lax.all_gather(forward_keys_own, "ctx", axis=1, tiled=True),
                lax.all_gather(forward_values_own, "ctx", axis=1, tiled=True),
            ),
        )
        heads_out = accum / denom[..., None]
        forward_lse = best + jnp.log(denom)
        forward_attn_f32 = jnp.transpose(heads_out, (0, 2, 1, 3))
        forward_attn = forward_attn_f32.reshape(row_count, forward_width).astype(jnp.bfloat16)
        forward_mixed = forward_inputs + matmul(forward_attn, forward_out_full)
        forward_norm_m = crms(forward_mixed, forward_gain_two.astype(jnp.float32)).astype(
            jnp.bfloat16
        )
        forward_pre = matmul(forward_norm_m, forward_up_full)
        forward_act = gelu_tanh(forward_pre).astype(jnp.bfloat16)
        result = (forward_mixed + matmul(forward_act, forward_down_full)).reshape(
            seq_count, local_len, res_width
        )
        forward_saved = (
            forward_inputs,
            forward_seg_rows,
            forward_query_seg,
            forward_norm_a,
            forward_queries,
            forward_keys_own,
            forward_values_own,
            forward_attn_f32,
            forward_lse,
            forward_attn,
            forward_mixed,
            forward_norm_m,
            forward_pre,
            forward_act,
        )
        result, saved = (result, forward_saved)
        grad_inputs, grads = backward(number, fetch(), saved)
        outputs.append(result)
        input_grads.append(grad_inputs)
        shares = (
            lax.psum_scatter(grads[0], ("seq", "ctx"), scatter_dimension=0, tiled=True),
            lax.psum_scatter(grads[1], ("seq", "ctx"), scatter_dimension=0, tiled=True),
            lax.psum_scatter(grads[2], ("seq", "ctx"), scatter_dimension=0, tiled=True),
            lax.psum_scatter(grads[3], ("seq", "ctx"), scatter_dimension=0, tiled=True),
            lax.psum_scatter(grads[4], ("seq", "ctx"), scatter_dimension=0, tiled=True),
            lax.psum_scatter(grads[5], ("seq", "ctx"), scatter_dimension=0, tiled=True),
        )
        owned = shares if owned is None else jax.tree.map(jnp.add, owned, shares)
    return (jnp.stack(outputs), jnp.stack(input_grads)) + tuple(owned)


SLOTS = 10
LOCAL = 96
WINDOW = 768
ROWS = 3 * LOCAL
KEYS = SLOTS * LOCAL
Z_SHIFT = [[(i, (i + 2 * k) % 8) for i in range(8)] for k in range(4)]
Y_SWAP = [(i, i ^ 1) for i in range(8)]
X_SWAP = [(i, i ^ 2) for i in range(4)]
CORE_SWAP = [(i, i ^ 1) for i in range(4)]


def make_plan():
    low = {d: 2 for d in range(8)}
    low[2], low[5] = 1, 0
    edges = [(d, f) for d in (5, 2, 7, 4, 1, 6, 3, 0) for f in range(8 * (3 * d // 8), 3 * d)]
    slot = {}

    def place(n):
        if n == len(edges):
            return True
        d, f = edges[n]
        for s in range(low[d], 7):
            if not any(t == s and (e == d or (g - f) % 8 == 0) for (e, g), t in slot.items()):
                slot[d, f] = s
                if place(n + 1):
                    return True
                del slot[d, f]
        return False

    assert place(0)
    for d in range(8):
        for j in range(3):
            slot[d, 3 * d + j] = 7 + j
    return slot


SLOT_OF = make_plan()
FLAT_AT = np.full((8, SLOTS), -1, np.int32)
for (_d, _f), _s in SLOT_OF.items():
    FLAT_AT[_d, _s] = _f
PAIRS = [[(int(FLAT_AT[d, s]) % 8, d) for d in range(8) if FLAT_AT[d, s] >= 0] for s in range(SLOTS)]
SEND_MICRO = np.zeros((SLOTS, 8), np.int32)
for _s in range(SLOTS):
    for _d in range(8):
        if FLAT_AT[_d, _s] >= 0:
            SEND_MICRO[_s, FLAT_AT[_d, _s] % 8] = FLAT_AT[_d, _s] // 8
STARTS = np.full((8, 3), 2 * LOCAL, np.int32)
STARTS[2] = (LOCAL, LOCAL, 2 * LOCAL)
STARTS[5] = (0, 2 * LOCAL, 2 * LOCAL)
ROUND_OF = np.array([[(8 * m + c) % 3 for m in range(3)] for c in range(8)], np.int32)
BACK = {
    shift: np.array(
        [
            [SLOT_OF.get((d, 3 * (d - shift) + j), -1) if d >= shift else -1 for j in range(3)]
            for d in range(8)
        ],
        np.int32,
    )
    for shift in (1, 2, 3)
}


def swap_seq(array, pairs):
    return lax.ppermute(array, "seq", pairs)


def swap_ctx(array, pairs):
    return lax.ppermute(array, "ctx", pairs)


def spread(own, x_first):
    seq, ctx = lax.axis_index("seq"), lax.axis_index("ctx")
    x, core, z, y = seq // 2, seq % 2, ctx // 2, ctx % 2
    rows, columns = own.shape
    line = jnp.zeros((4, rows, columns), own.dtype)
    for k in range(4):
        piece = own if k == 0 else swap_ctx(own, Z_SHIFT[k])
        line = lax.dynamic_update_index_in_dim(line, piece, (z - k) % 4, 0)
    line_x = swap_seq(line, X_SWAP)
    line_y = swap_ctx(line, Y_SWAP)
    line_xy = swap_ctx(line_x, Y_SWAP) if x_first else swap_seq(line_y, X_SWAP)
    full = jnp.zeros((2, 2, 4, 2, rows, columns), own.dtype)
    for piece, px, py in ((line, x, y), (line_x, 1 - x, y), (line_y, x, 1 - y), (line_xy, 1 - x, 1 - y)):
        other = swap_seq(piece, CORE_SWAP)
        for part, pc in ((piece, core), (other, 1 - core)):
            full = lax.dynamic_update_slice(
                full, part[None, None, :, None], (px, pc, 0, py, 0, 0)
            )
    return full.reshape(32 * rows, columns)


def pick(array, index, axis):
    return lax.dynamic_index_in_dim(array, index, axis, keepdims=False)


def add_low(left, right):
    return (left.astype(jnp.float32) + right.astype(jnp.float32)).astype(jnp.bfloat16)


def collect(part, y_first):
    seq, ctx = lax.axis_index("seq"), lax.axis_index("ctx")
    x, core, z, y = seq // 2, seq % 2, ctx // 2, ctx % 2
    rows, columns = part.shape[0] // 32, part.shape[1]
    part = part.reshape(2, 2, 4, 2, rows, columns)
    held = add_low(pick(part, core, 1), swap_seq(pick(part, 1 - core, 1), CORE_SWAP))
    if y_first:
        held = add_low(pick(held, y, 2), swap_ctx(pick(held, 1 - y, 2), Y_SWAP))
        held = add_low(pick(held, x, 0), swap_seq(pick(held, 1 - x, 0), X_SWAP))
    else:
        held = add_low(pick(held, x, 0), swap_seq(pick(held, 1 - x, 0), X_SWAP))
        held = add_low(pick(held, y, 1), swap_ctx(pick(held, 1 - y, 1), Y_SWAP))
    total = pick(held, z, 0).astype(jnp.float32)
    for k in range(1, 4):
        total = total + swap_ctx(pick(held, (z + k) % 4, 0), Z_SHIFT[k]).astype(jnp.float32)
    return total


def norm_parts(rows):
    width = rows.shape[-1]
    totals = jnp.sum(rows, axis=-1, keepdims=True)
    meansq = (jnp.sum(rows * rows, axis=-1, keepdims=True) + totals * totals) / width
    scale = lax.rsqrt(meansq + EPS)
    last = lax.broadcasted_iota(jnp.int32, rows.shape, 1) == width - 1
    return jnp.where(last, -totals, rows) * scale, scale


def norm_back(normed, scale, gains, grads):
    width = normed.shape[-1]
    weighted = grads * gains
    mean = jnp.sum(weighted * normed, axis=-1, keepdims=True) / width
    grad_u = scale * (weighted - normed * mean)
    last = lax.broadcasted_iota(jnp.int32, grad_u.shape, 1) == width - 1
    final = jnp.sum(jnp.where(last, grad_u, 0.0), axis=-1, keepdims=True)
    return jnp.where(last, 0.0, grad_u - final)


def stack_heads(block):
    head = lax.broadcasted_iota(jnp.int32, block.shape, 1) // HEAD_DIM
    return jnp.concatenate([jnp.where(head == i, block, jnp.zeros_like(block)) for i in range(4)], axis=0)


def unstack_heads(turned):
    rows = turned.T
    head = lax.broadcasted_iota(jnp.int32, (LOCAL, 4 * HEAD_DIM), 1) // HEAD_DIM
    picked = rows[:LOCAL]
    for i in range(1, 4):
        picked = jnp.where(head == i, rows[i * LOCAL : (i + 1) * LOCAL], picked)
    return picked


def attend_kernel(starts, q_ref, k_ref, v_ref, key_ref, query_ref, out_ref, probs_ref, bias_ref):
    window = pl.ds(pl.multiple_of(starts[pl.program_id(0)], 32), WINDOW)

    @pl.when(pl.program_id(1) == 0)
    def _():
        same = key_ref[window, 0:1] == query_ref[0, 0:1, :]
        causal = key_ref[window, 1:2] <= query_ref[0, 1:2, :]
        bias_ref[...] = jnp.where(same & causal, 0.0, NEG)

    stacked = stack_heads(q_ref[...])
    scores = matmul_right_t(k_ref[window, :], stacked) + bias_ref[...]
    weights = jnp.exp(scores - jnp.max(scores, axis=0, keepdims=True))
    probs = (weights * (1.0 / jnp.sum(weights, axis=0, keepdims=True))).astype(jnp.bfloat16)
    probs_ref[0, 0] = probs
    out_ref[...] = unstack_heads(matmul(v_ref[window, :].T, probs)).astype(jnp.bfloat16)


def attend(queries, keys, values, starts, key_marks, query_marks):
    return pl.pallas_call(
        attend_kernel,
        grid_spec=pltpu.PrefetchScalarGridSpec(
            num_scalar_prefetch=1,
            grid=(3, 3),
            in_specs=[
                pl.BlockSpec((LOCAL, 256), lambda j, h, s: (j, h)),
                pl.BlockSpec((KEYS, 256), lambda j, h, s: (0, h)),
                pl.BlockSpec((KEYS, 256), lambda j, h, s: (0, h)),
                pl.BlockSpec((KEYS, 2), lambda j, h, s: (0, 0)),
                pl.BlockSpec((1, 2, 4 * LOCAL), lambda j, h, s: (j, 0, 0)),
            ],
            out_specs=[
                pl.BlockSpec((LOCAL, 256), lambda j, h, s: (j, h)),
                pl.BlockSpec((1, 1, WINDOW, 4 * LOCAL), lambda j, h, s: (j, h, 0, 0)),
            ],
            scratch_shapes=[pltpu.VMEM((WINDOW, 4 * LOCAL), jnp.float32)],
        ),
        out_shape=[
            jax.ShapeDtypeStruct((ROWS, 768), jnp.bfloat16),
            jax.ShapeDtypeStruct((3, 3, WINDOW, 4 * LOCAL), jnp.bfloat16),
        ],
        compiler_params=pltpu.CompilerParams(vmem_limit_bytes=40 * 1024 * 1024),
        cost_estimate=pl.CostEstimate(flops=3_000_000_000, bytes_accessed=12_000_000, transcendentals=2_700_000),
        name="attend",
    )(starts, queries, keys, values, key_marks, query_marks)


def attend_back_kernel(
    starts, q_ref, k_ref, v_ref, grad_ref, probs_ref, grad_q_ref, grad_k_ref, grad_v_ref, sum_k, sum_v
):
    row_block = pl.program_id(1)
    window = pl.ds(pl.multiple_of(starts[row_block], 32), WINDOW)

    @pl.when(row_block == 0)
    def _():
        sum_k[...] = jnp.zeros_like(sum_k)
        sum_v[...] = jnp.zeros_like(sum_v)

    probs = probs_ref[0, 0]
    grads = stack_heads(grad_ref[...])
    wide = probs.astype(jnp.float32)
    terms = wide * matmul_right_t(v_ref[window, :], grads)
    grad_scores = (terms - wide * jnp.sum(terms, axis=0, keepdims=True)).astype(jnp.bfloat16)
    sum_v[window, :] += matmul(probs, grads)
    sum_k[window, :] += matmul(grad_scores, stack_heads(q_ref[...]))
    grad_q = unstack_heads(matmul(k_ref[window, :].T, grad_scores)) * SCALE
    grad_q_ref[...] = grad_q.astype(jnp.bfloat16)

    @pl.when(row_block == 2)
    def _():
        grad_k_ref[...] = sum_k[...].astype(jnp.bfloat16)
        grad_v_ref[...] = sum_v[...].astype(jnp.bfloat16)


def attend_back(queries, keys, values, grads, probs, starts):
    return pl.pallas_call(
        attend_back_kernel,
        grid_spec=pltpu.PrefetchScalarGridSpec(
            num_scalar_prefetch=1,
            grid=(3, 3),
            in_specs=[
                pl.BlockSpec((LOCAL, 256), lambda h, j, s: (j, h)),
                pl.BlockSpec((KEYS, 256), lambda h, j, s: (0, h)),
                pl.BlockSpec((KEYS, 256), lambda h, j, s: (0, h)),
                pl.BlockSpec((LOCAL, 256), lambda h, j, s: (j, h)),
                pl.BlockSpec((1, 1, WINDOW, 4 * LOCAL), lambda h, j, s: (j, h, 0, 0)),
            ],
            out_specs=[
                pl.BlockSpec((LOCAL, 256), lambda h, j, s: (j, h)),
                pl.BlockSpec((KEYS, 256), lambda h, j, s: (0, h)),
                pl.BlockSpec((KEYS, 256), lambda h, j, s: (0, h)),
            ],
            scratch_shapes=[pltpu.VMEM((KEYS, 256), jnp.float32), pltpu.VMEM((KEYS, 256), jnp.float32)],
        ),
        out_shape=[
            jax.ShapeDtypeStruct((ROWS, 768), jnp.bfloat16),
            jax.ShapeDtypeStruct((KEYS, 768), jnp.bfloat16),
            jax.ShapeDtypeStruct((KEYS, 768), jnp.bfloat16),
        ],
        compiler_params=pltpu.CompilerParams(vmem_limit_bytes=40 * 1024 * 1024),
        cost_estimate=pl.CostEstimate(flops=7_000_000_000, bytes_accessed=14_000_000, transcendentals=0),
        name="attend_back",
    )(starts, queries, keys, values, grads, probs)


def widen(array):
    return jnp.pad(array, [(0, 0)] * (array.ndim - 1) + [(0, 1)])


def hand_back(delta, base, ctx):
    delta = delta.astype(jnp.bfloat16).reshape(3, LOCAL, -1)
    parts = jnp.stack(
        [swap_ctx(delta[j], [(d, (3 * d + j) % 8) for d in range(8)]) for j in range(3)]
    )
    order = jnp.asarray(ROUND_OF)[ctx]
    home = jnp.stack([pick(parts, order[m], 0) for m in range(3)])
    return base.astype(jnp.float32) + home[..., : base.shape[-1]].astype(jnp.float32)


def spread_body(
    tokens,
    segment_ids,
    qkv_weight,
    out_weight,
    up_weight,
    down_weight,
    attn_gain,
    mlp_gain,
    out_cotangent,
):
    micro_count, _, local_len, res_width = tokens.shape
    width = res_width + 1
    ctx = lax.axis_index("ctx")
    tokens = tokens.reshape(micro_count, local_len, res_width)
    cotangent = out_cotangent.reshape(micro_count, local_len, res_width)

    def rounds(array, slots):
        wide = widen(array)
        micro_of = jnp.asarray(SEND_MICRO)[:, ctx]
        return jnp.concatenate(
            [swap_ctx(pick(wide, micro_of[s], 0), PAIRS[s]) for s in slots], axis=0
        )

    key_rows = rounds(tokens, range(SLOTS)).astype(jnp.float32)
    gains_own = jnp.pad(jnp.stack([attn_gain, mlp_gain], axis=1), ((0, 0), (0, 126)))
    first = spread(jnp.concatenate([qkv_weight[:, :width], widen(out_weight), gains_own], axis=1), True)
    second = spread(qkv_weight[:, width:], False)
    up_full = spread(up_weight, True)
    down_full = spread(widen(down_weight), False)
    grad_rows = rounds(cotangent, range(7, SLOTS))
    q_full, out_full = first[:, :width], first[:, width : 2 * width]
    gain_one = first[:, 2 * width].astype(jnp.float32)
    gain_two = first[:, 2 * width + 1].astype(jnp.float32)

    flat_at = jnp.asarray(FLAT_AT)[ctx]
    ids = segment_ids.reshape(micro_count, -1) + 8 * jnp.arange(micro_count, dtype=jnp.int32)[:, None]
    ids = ids.reshape(-1, local_len)
    ids = jnp.stack([jnp.where(flat_at[s] >= 0, pick(ids, jnp.maximum(flat_at[s], 0), 0), -1) for s in range(SLOTS)])
    places = flat_at[:, None] * local_len + jnp.arange(local_len, dtype=jnp.int32)[None, :]
    key_marks = jnp.stack([ids.reshape(-1), places.reshape(-1)], axis=1)
    query_marks = jnp.stack([jnp.tile(ids[7:], (1, 4)), jnp.tile(places[7:], (1, 4))], axis=1)
    starts = jnp.asarray(STARTS)[ctx]

    inputs = key_rows[KEYS - ROWS :]
    key_normed, key_scale = norm_parts(key_rows)
    norm_keys = (key_normed * gain_one).astype(jnp.bfloat16)
    norm_a = norm_keys[KEYS - ROWS :]
    queries = (matmul(norm_a, q_full).astype(jnp.bfloat16) * SCALE).astype(jnp.bfloat16)
    keys_values = matmul(norm_keys, second).astype(jnp.bfloat16)
    keys, values = keys_values[:, :width], keys_values[:, width:]
    attn, probs = attend(queries, keys, values, starts, key_marks, query_marks)
    branch = matmul(attn, out_full)
    mixed = inputs + branch
    mixed_normed, mixed_scale = norm_parts(mixed)
    norm_m = (mixed_normed * gain_two).astype(jnp.bfloat16)
    pre = matmul(norm_m, up_full)
    act, gelu_pull = jax.vjp(gelu_tanh, pre)
    act = act.astype(jnp.bfloat16)
    result = hand_back(branch + matmul(act, down_full), tokens, ctx)

    grad_down = collect(matmul_left_t(act, grad_rows).astype(jnp.bfloat16), True)
    grad_pre = gelu_pull(matmul_right_t(grad_rows, down_full))[0].astype(jnp.bfloat16)
    grad_up = collect(matmul_left_t(norm_m, grad_pre).astype(jnp.bfloat16), False)
    grad_norm_m = matmul_right_t(grad_pre, up_full)
    grad_mixed_norm = norm_back(mixed_normed, mixed_scale, gain_two, grad_norm_m)
    grad_branch = (grad_rows.astype(jnp.float32) + grad_mixed_norm).astype(jnp.bfloat16)
    grad_out = matmul_left_t(attn, grad_branch).astype(jnp.bfloat16)
    grad_attn = matmul_right_t(grad_branch, out_full).astype(jnp.bfloat16)
    grad_q, grad_k, grad_v = attend_back(queries, keys, values, grad_attn, probs, starts)
    grad_kv = jnp.concatenate([grad_k, grad_v], axis=1)
    grad_norm_keys = matmul_right_t(grad_kv, second)
    grad_norm_a = grad_norm_keys[KEYS - ROWS :] + matmul_right_t(grad_q, q_full)
    for shift, blocks in ((1, (0, 1, 2)), (2, (0, 1, 2)), (3, (2,))):
        table = jnp.asarray(BACK[shift])[ctx]
        sent = jnp.concatenate(
            [
                jnp.where(
                    table[j] >= 0,
                    lax.dynamic_slice_in_dim(grad_norm_keys, jnp.maximum(table[j], 0) * local_len, local_len, 0),
                    0.0,
                ).astype(jnp.bfloat16)
                for j in blocks
            ],
            axis=0,
        )
        pairs = [(d, d - shift) for d in range(8) if any(BACK[shift][d, j] >= 0 for j in range(3))]
        back = swap_ctx(sent, pairs).astype(jnp.float32)
        grad_norm_a = grad_norm_a + jnp.pad(back, ((blocks[0] * local_len, 0), (0, 0)))
    grad_q_out = jnp.concatenate([matmul_left_t(norm_a, grad_q).astype(jnp.bfloat16), grad_out], axis=1)
    grad_q_out = collect(grad_q_out, False)
    grad_kv_weight = collect(matmul_left_t(norm_keys, grad_kv).astype(jnp.bfloat16), True)
    grad_input_norm = norm_back(
        key_normed[KEYS - ROWS :], key_scale[KEYS - ROWS :], gain_one, grad_norm_a
    )
    grad_tokens = hand_back(grad_mixed_norm + grad_input_norm, cotangent, ctx)
    grad_qkv = jnp.concatenate([grad_q_out[:, :width], grad_kv_weight], axis=1)
    grad_gain_one = jnp.sum(qkv_weight.astype(jnp.float32) * grad_qkv, axis=1) / attn_gain.astype(jnp.float32)
    grad_gain_two = jnp.sum(up_weight.astype(jnp.float32) * grad_up, axis=1) / mlp_gain.astype(jnp.float32)
    shape = (micro_count, 1, local_len, res_width)
    return (
        result.reshape(shape),
        grad_tokens.reshape(shape),
        grad_qkv,
        grad_q_out[:, width : 2 * width - 1],
        grad_up,
        grad_down[:, :res_width],
        grad_gain_one,
        grad_gain_two,
    )


def solution(mesh):
    small = (mesh.shape["seq"], mesh.shape["ctx"]) == (4, 8)
    return jax.shard_map(
        spread_body if small else body,
        mesh=mesh,
        in_specs=(
            P(None, "seq", "ctx", None),
            P(None, "seq", None),
            P(("seq", "ctx"), None),
            P(("seq", "ctx"), None),
            P(("seq", "ctx"), None),
            P(("seq", "ctx"), None),
            P(("seq", "ctx")),
            P(("seq", "ctx")),
            P(None, "seq", "ctx", None),
        ),
        out_specs=(
            P(None, "seq", "ctx", None),
            P(None, "seq", "ctx", None),
            P(("seq", "ctx"), None),
            P(("seq", "ctx"), None),
            P(("seq", "ctx"), None),
            P(("seq", "ctx"), None),
            P(("seq", "ctx")),
            P(("seq", "ctx")),
        ),
        check_vma=False,
    )
```

```python
import functools
import math

import jax
import jax.numpy as jnp
import numpy as np
from jax import lax
from jax.experimental import pallas as pl
from jax.experimental.pallas import tpu as pltpu
from jax.sharding import PartitionSpec as P

HEADS = 12
HEAD_DIM = 64


EPS = 1e-05
NEG = -1e30
SCALE = 0.125


def crms(inputs, gains):
    totals = jnp.sum(inputs, axis=-1, keepdims=True)
    meansq = (jnp.sum(inputs * inputs, axis=-1, keepdims=True) + totals * totals) / gains.shape[0]
    return jnp.concatenate([inputs, -totals], axis=-1) * lax.rsqrt(meansq + EPS) * gains


def gelu_tanh(inputs):
    return jax.nn.gelu(inputs, approximate=True)


def matmul(left, right):
    return jnp.dot(left, right, preferred_element_type=jnp.float32)


def matmul_left_t(left, right):
    return lax.dot_general(
        left, right, (((0,), (0,)), ((), ())), preferred_element_type=jnp.float32
    )


def matmul_right_t(left, right):
    return lax.dot_general(
        left, right, (((1,), (1,)), ((), ())), preferred_element_type=jnp.float32
    )


def allowed_pairs(query_pos, query_seg, key_pos, key_seg):
    same_doc = query_seg[:, None, :, None] == key_seg[:, None, None, :]
    causal = query_pos[None, None, :, None] >= key_pos[None, None, None, :]
    return same_doc & causal


def attend_block(state, queries, query_pos, query_seg, keys, values, key_pos, key_seg):
    best, denom, accum = state
    scores = (
        jnp.einsum("bqhd,bkhd->bhqk", queries, keys, preferred_element_type=jnp.float32) * SCALE
    )
    allowed = allowed_pairs(query_pos, query_seg, key_pos, key_seg)
    scores = jnp.where(allowed, scores, NEG)
    peak = jnp.maximum(best, jnp.max(scores, axis=-1))
    weights = jnp.where(allowed, jnp.exp(scores - peak[..., None]), 0.0)
    factor = jnp.exp(best - peak)
    denom = denom * factor + jnp.sum(weights, axis=-1)
    accum = accum * factor[..., None] + jnp.einsum(
        "bhqk,bkhd->bhqd", weights.astype(jnp.bfloat16), values, preferred_element_type=jnp.float32
    )
    return (peak, denom, accum)


def pair_grads(queries, grad_o, lse, delta, query_pos, query_seg, keys, values, key_pos, key_seg):
    scores = (
        jnp.einsum("bqhd,bkhd->bhqk", queries, keys, preferred_element_type=jnp.float32) * SCALE
    )
    allowed = allowed_pairs(query_pos, query_seg, key_pos, key_seg)
    probs = jnp.where(allowed, jnp.exp(scores - lse[..., None]), 0.0)
    dprobs = jnp.einsum("bqhd,bkhd->bhqk", grad_o, values, preferred_element_type=jnp.float32)
    grad_scores = (probs * (dprobs - delta[..., None])).astype(jnp.bfloat16)
    part_q = (
        jnp.einsum("bhqk,bkhd->bqhd", grad_scores, keys, preferred_element_type=jnp.float32) * SCALE
    )
    part_k = (
        jnp.einsum("bhqk,bqhd->bkhd", grad_scores, queries, preferred_element_type=jnp.float32)
        * SCALE
    )
    part_v = jnp.einsum(
        "bhqk,bqhd->bkhd", probs.astype(jnp.bfloat16), grad_o, preferred_element_type=jnp.float32
    )
    return (part_q, part_k, part_v)


def body(
    tokens,
    segment_ids,
    qkv_weight,
    out_weight,
    up_weight,
    down_weight,
    attn_gain,
    mlp_gain,
    out_cotangent,
):
    micro_count, seq_count, local_len, res_width = tokens.shape
    length = segment_ids.shape[2]
    first = lax.axis_index("ctx") * local_len
    query_pos = first + jnp.arange(local_len, dtype=jnp.int32)
    row_count = seq_count * local_len

    def fetch():
        return (
            lax.all_gather(qkv_weight, ("seq", "ctx"), axis=0, tiled=True),
            lax.all_gather(out_weight, ("seq", "ctx"), axis=0, tiled=True),
            lax.all_gather(up_weight, ("seq", "ctx"), axis=0, tiled=True),
            lax.all_gather(down_weight, ("seq", "ctx"), axis=0, tiled=True),
            lax.all_gather(attn_gain, ("seq", "ctx"), axis=0, tiled=True),
            lax.all_gather(mlp_gain, ("seq", "ctx"), axis=0, tiled=True),
        )

    def backward(number, gathered, saved):
        qkv_full, out_full, up_full, down_full, gain_one, gain_two = gathered
        (
            inputs,
            seg_rows,
            query_seg,
            norm_a,
            queries,
            keys_own,
            values_own,
            attn_f32,
            lse,
            attn,
            mixed,
            norm_m,
            pre,
            act,
        ) = saved
        width = qkv_full.shape[0]
        grad_y = out_cotangent[number].reshape(row_count, res_width)
        grad_down = matmul_left_t(act, grad_y)
        grad_act = matmul_right_t(grad_y, down_full)
        _, gelu_pull = jax.vjp(gelu_tanh, pre)
        grad_pre = gelu_pull(grad_act)[0].astype(jnp.bfloat16)
        grad_up = matmul_left_t(norm_m, grad_pre)
        grad_norm_m = matmul_right_t(grad_pre, up_full)
        _, pull_two = jax.vjp(crms, mixed, gain_two.astype(jnp.float32))
        grad_mixed_norm, grad_gain_two = pull_two(grad_norm_m)
        grad_mixed = grad_y.astype(jnp.float32) + grad_mixed_norm
        grad_branch = grad_mixed.astype(jnp.bfloat16)
        grad_outw = matmul_left_t(attn, grad_branch)
        grad_attn = (
            matmul_right_t(grad_branch, out_full)
            .astype(jnp.bfloat16)
            .reshape(seq_count, local_len, HEADS, HEAD_DIM)
        )
        delta = jnp.transpose(jnp.sum(grad_attn.astype(jnp.float32) * attn_f32, axis=-1), (0, 2, 1))
        block_len = math.gcd(length, 1024)
        block_ids = jnp.arange(length // block_len, dtype=jnp.int32)
        keys_all, values_all = (
            lax.all_gather(keys_own, "ctx", axis=1, tiled=True),
            lax.all_gather(values_own, "ctx", axis=1, tiled=True),
        )

        def back_keys(carry, number_block):
            offset = number_block * block_len
            key_block = lax.dynamic_slice_in_dim(keys_all, offset, block_len, 1)
            value_block = lax.dynamic_slice_in_dim(values_all, offset, block_len, 1)
            key_pos = offset + jnp.arange(block_len, dtype=jnp.int32)
            key_seg = lax.dynamic_slice_in_dim(seg_rows, offset, block_len, 1)
            part_q, part_k, part_v = pair_grads(
                queries,
                grad_attn,
                lse,
                delta,
                query_pos,
                query_seg,
                key_block,
                value_block,
                key_pos,
                key_seg,
            )
            return (carry + part_q, jnp.concatenate([part_k, part_v], axis=-1))

        grad_q, terms = lax.scan(back_keys, jnp.zeros(queries.shape, jnp.float32), block_ids)
        terms = jnp.moveaxis(terms, 0, 1).reshape(seq_count, length, HEADS, 2 * HEAD_DIM)
        owned_terms = lax.psum_scatter(terms, "ctx", scatter_dimension=1, tiled=True)
        grad_k = owned_terms[..., :HEAD_DIM]
        grad_v = owned_terms[..., HEAD_DIM:]
        grad_qkv = jnp.concatenate(
            [
                grad_q.reshape(row_count, width),
                grad_k.reshape(row_count, width),
                grad_v.reshape(row_count, width),
            ],
            axis=-1,
        ).astype(jnp.bfloat16)
        grad_qkvw = matmul_left_t(norm_a, grad_qkv)
        grad_norm_a = matmul_right_t(grad_qkv, qkv_full)
        _, pull_one = jax.vjp(crms, inputs, gain_one.astype(jnp.float32))
        grad_input_norm, grad_gain_one = pull_one(grad_norm_a)
        grad_inputs = (grad_mixed + grad_input_norm).reshape(seq_count, local_len, res_width)
        return (
            grad_inputs,
            (grad_qkvw, grad_outw, grad_up, grad_down, grad_gain_one, grad_gain_two),
        )

    outputs = []
    input_grads = []
    owned = None
    for number in range(micro_count):
        (
            forward_qkv_full,
            forward_out_full,
            forward_up_full,
            forward_down_full,
            forward_gain_one,
            forward_gain_two,
        ) = fetch()
        forward_width = forward_qkv_full.shape[0]
        forward_inputs = tokens[number].astype(jnp.float32).reshape(row_count, res_width)
        forward_seg_rows = segment_ids[number]
        forward_query_seg = lax.dynamic_slice_in_dim(forward_seg_rows, first, local_len, 1)
        forward_norm_a = crms(forward_inputs, forward_gain_one.astype(jnp.float32)).astype(
            jnp.bfloat16
        )
        qkv = matmul(forward_norm_a, forward_qkv_full).astype(jnp.bfloat16)
        forward_queries = qkv[:, :forward_width].reshape(seq_count, local_len, HEADS, HEAD_DIM)
        forward_keys_own = qkv[:, forward_width : 2 * forward_width].reshape(
            seq_count, local_len, HEADS, HEAD_DIM
        )
        forward_values_own = qkv[:, 2 * forward_width :].reshape(
            seq_count, local_len, HEADS, HEAD_DIM
        )

        def fold_keys(state, piece):
            keys_part, values_part = piece
            span = keys_part.shape[1]
            block_len = span if span <= 1024 else math.gcd(span, 1024)

            def inner(carry, number_block):
                offset = number_block * block_len
                key_block = lax.dynamic_slice_in_dim(keys_part, offset, block_len, 1)
                value_block = lax.dynamic_slice_in_dim(values_part, offset, block_len, 1)
                key_pos = offset + jnp.arange(block_len, dtype=jnp.int32)
                key_seg = lax.dynamic_slice_in_dim(forward_seg_rows, offset, block_len, 1)
                return (
                    attend_block(
                        carry,
                        forward_queries,
                        query_pos,
                        forward_query_seg,
                        key_block,
                        value_block,
                        key_pos,
                        key_seg,
                    ),
                    None,
                )

            state, _ = lax.scan(inner, state, jnp.arange(span // block_len, dtype=jnp.int32))
            return state

        initial = (
            jnp.full((seq_count, HEADS, local_len), NEG, jnp.float32),
            jnp.zeros((seq_count, HEADS, local_len), jnp.float32),
            jnp.zeros((seq_count, HEADS, local_len, HEAD_DIM), jnp.float32),
        )
        best, denom, accum = fold_keys(
            initial,
            (
                lax.all_gather(forward_keys_own, "ctx", axis=1, tiled=True),
                lax.all_gather(forward_values_own, "ctx", axis=1, tiled=True),
            ),
        )
        heads_out = accum / denom[..., None]
        forward_lse = best + jnp.log(denom)
        forward_attn_f32 = jnp.transpose(heads_out, (0, 2, 1, 3))
        forward_attn = forward_attn_f32.reshape(row_count, forward_width).astype(jnp.bfloat16)
        forward_mixed = forward_inputs + matmul(forward_attn, forward_out_full)
        forward_norm_m = crms(forward_mixed, forward_gain_two.astype(jnp.float32)).astype(
            jnp.bfloat16
        )
        forward_pre = matmul(forward_norm_m, forward_up_full)
        forward_act = gelu_tanh(forward_pre).astype(jnp.bfloat16)
        result = (forward_mixed + matmul(forward_act, forward_down_full)).reshape(
            seq_count, local_len, res_width
        )
        forward_saved = (
            forward_inputs,
            forward_seg_rows,
            forward_query_seg,
            forward_norm_a,
            forward_queries,
            forward_keys_own,
            forward_values_own,
            forward_attn_f32,
            forward_lse,
            forward_attn,
            forward_mixed,
            forward_norm_m,
            forward_pre,
            forward_act,
        )
        result, saved = (result, forward_saved)
        grad_inputs, grads = backward(number, fetch(), saved)
        outputs.append(result)
        input_grads.append(grad_inputs)
        shares = (
            lax.psum_scatter(grads[0], ("seq", "ctx"), scatter_dimension=0, tiled=True),
            lax.psum_scatter(grads[1], ("seq", "ctx"), scatter_dimension=0, tiled=True),
            lax.psum_scatter(grads[2], ("seq", "ctx"), scatter_dimension=0, tiled=True),
            lax.psum_scatter(grads[3], ("seq", "ctx"), scatter_dimension=0, tiled=True),
            lax.psum_scatter(grads[4], ("seq", "ctx"), scatter_dimension=0, tiled=True),
            lax.psum_scatter(grads[5], ("seq", "ctx"), scatter_dimension=0, tiled=True),
        )
        owned = shares if owned is None else jax.tree.map(jnp.add, owned, shares)
    return (jnp.stack(outputs), jnp.stack(input_grads)) + tuple(owned)


FLAGS = {'deal': 3, 'cut': 1280, 'shift': 1, 'f0': 0, 'f1': 1, 'f2': 1, 'f3': 1, 'f4': 0, 'f5': 1, 'f6': 1, 'f7': 0, 'f8': 0, 'home': 0, 'b0': 1, 'b1': 0, 'b2': 1, 'b3': 1, 'b4': 0, 'b5': 0, 'b6': 1, 'b7': 0, 'outin': 1, 'dz': 0, 'c': 0, 'dxfirst': 0, 'lz': 0, 'ez': 0, 'dfold': 0, 'ufold': 0, 'upfirst': 1}
SLOTS = 10
LOCAL = 96
WINDOW = 768
ROWS = 3 * LOCAL
KEYS = SLOTS * LOCAL
Z_SWAP = [(i, i ^ 2) for i in range(8)]
Z_FAR = [(i, i ^ 4) for i in range(8)]
Z_SHIFT = [[(i, (i + 2 * k) % 8) for i in range(8)] for k in range(4)]
Y_SWAP = [(i, i ^ 1) for i in range(8)]
X_SWAP = [(i, i ^ 2) for i in range(4)]
CORE_SWAP = [(i, i ^ 1) for i in range(4)]
DEAL = [[(f % 8, f // 3) for f in range(24) if f % 3 == j] for j in range(3)]
RETURN = [[(f // 3, f % 8) for f in range(24) if f % 3 == j] for j in range(3)]
UP = ([(d, d + 1) for d in range(7)], [(0, 2), (2, 4), (3, 5), (5, 7)], [(2, 5)])


def swap_seq(array, pairs):
    return lax.ppermute(array, "seq", pairs)


def swap_ctx(array, pairs):
    return lax.ppermute(array, "ctx", pairs)


def after(value, *others):
    return lax.optimization_barrier((value, others))[0]


def grid_place():
    seq, ctx = lax.axis_index("seq"), lax.axis_index("ctx")
    return seq // 2, seq % 2, ctx // 2, ctx % 2


def along_z(own, *others):
    pair = jnp.stack([own, swap_ctx(own, Z_FAR)])
    return jnp.stack([pair, swap_ctx(after(pair, *others), Z_SWAP)])


def plane_start(line, split):
    left, right = line[..., :split], line[..., split:]
    return jnp.stack([left, swap_seq(left, X_SWAP)]), jnp.stack([right, swap_ctx(right, Y_SWAP)])


def plane_end(left, right):
    return swap_ctx(left, Y_SWAP), swap_seq(right, X_SWAP)


def other_core(pieces):
    return [swap_seq(piece, CORE_SWAP) for piece in pieces]


def place_kernel(cuts, *refs):
    pieces, out_refs, sems = refs[:8], refs[8:-1], refs[-1]
    x, core, z, y = grid_place()
    copies = []
    for i, piece in enumerate(pieces):
        pc = core if i < 4 else 1 - core
        left, far = i % 4 in (0, 2), i % 4 >= 2
        for near in range(2):
            dx, dy = (near, far) if left else (far, near)
            px = 1 - x if dx else x
            py = 1 - y if dy else y
            for low in range(2):
                for high in range(2):
                    pz = z if low == 0 else z + 1 - 2 * (z % 2)
                    pz = pz if high == 0 else (pz + 2) % 4
                    for start, size, out, place in cuts[0 if left else 1]:
                        source = piece.at[near, low, high, :, pl.ds(start, size)]
                        target = out_refs[out].at[px, pc, pz, py]
                        target = target.at[place] if out else target.at[:, pl.ds(place, size)]
                        copies.append((source, target))
    copies = [pltpu.make_async_copy(*ends, sems.at[i]) for i, ends in enumerate(copies)]
    for copy in copies:
        copy.start()
    for copy in copies:
        copy.wait()


def all_rows(own, other, columns, blocks, split, width):
    rows = own[0].shape[-2]
    cuts = ([], [])
    for low, high, side in ((0, split, 0), (split, columns + blocks * width, 1)):
        start, end = low, min(high, columns)
        if end > start:
            cuts[side].append((start - low, end - start, 0, start))
        for block in range(blocks):
            if low <= columns + block * width < high:
                cuts[side].append((columns + block * width - low, width, 1, block))
    shapes = [jax.ShapeDtypeStruct((2, 2, 4, 2, rows, columns), own[0].dtype)]
    if blocks:
        shapes.append(jax.ShapeDtypeStruct((2, 2, 4, 2, blocks, rows, width), own[0].dtype))
    full = pl.pallas_call(
        functools.partial(place_kernel, cuts),
        in_specs=[pl.BlockSpec(memory_space=pltpu.HBM)] * 8,
        out_specs=[pl.BlockSpec(memory_space=pltpu.VMEM)] * len(shapes),
        out_shape=shapes,
        scratch_shapes=[pltpu.SemaphoreType.DMA((32 * (len(cuts[0]) + len(cuts[1])),))],
        compiler_params=pltpu.CompilerParams(vmem_limit_bytes=32 * 1024 * 1024),
        cost_estimate=pl.CostEstimate(
            flops=0, bytes_accessed=128 * rows * (columns + blocks * width), transcendentals=0
        ),
        name="place",
    )(*own, *other)
    return [full[0].reshape(32 * rows, columns)] + [part.reshape(32 * blocks * rows, width) for part in full[1:]]


def pick(array, index, axis):
    return lax.dynamic_index_in_dim(array, index, axis, keepdims=False)


def add_low(left, right):
    return (left.astype(jnp.float32) + right.astype(jnp.float32)).astype(jnp.bfloat16)


def core_rows(left, other):
    _, core, _, _ = grid_place()
    step = left.shape[1] // 4
    first, second, third, fourth = [left[:, i * step : (i + 1) * step] for i in range(4)]
    low = core == (1 if other else 0)
    return jnp.concatenate([jnp.where(low, first, second), jnp.where(low, third, fourth)], axis=1)


def fold_part(part):
    _, core, _, _ = grid_place()
    part = part.reshape(2, 2, 4, 2, -1, part.shape[-1])
    return add_low(pick(part, core, 1), swap_seq(pick(part, 1 - core, 1), CORE_SWAP))


def fold_send(left, right):
    return swap_seq(matmul_left_t(core_rows(left, True), right).astype(jnp.bfloat16), CORE_SWAP)


def fold_core(left, right, got):
    held = (matmul_left_t(core_rows(left, False), right) + got.astype(jnp.float32)).astype(jnp.bfloat16)
    return held.reshape(2, 4, 2, -1, held.shape[-1])


def fold_x(held):
    x, _, _, _ = grid_place()
    return add_low(pick(held, x, 0), swap_seq(pick(held, 1 - x, 0), X_SWAP))


def fold_y(held):
    _, _, _, y = grid_place()
    axis = held.ndim - 3
    return add_low(pick(held, y, axis), swap_ctx(pick(held, 1 - y, axis), Y_SWAP))


def fold_start(left, right):
    return fold_x(left), fold_y(right)


def fold_end(left, right):
    return jnp.concatenate([fold_y(left), fold_x(right)], axis=-1)


def halves(held):
    half = held.shape[-1] // 2
    return held[..., :half], held[..., half:]


def fold_z(line):
    _, _, z, _ = grid_place()
    total = pick(line, z, 0).astype(jnp.float32)
    for k in range(1, 4):
        total = total + swap_ctx(pick(line, (z + k) % 4, 0), Z_SHIFT[k]).astype(jnp.float32)
    return total


def fold_near_z(line):
    _, _, z, _ = grid_place()
    pairs = line.reshape((2, 2) + line.shape[1:])
    return add_low(pick(pairs, z % 2, 1), swap_ctx(pick(pairs, 1 - z % 2, 1), Z_SWAP))


def fold_far_z(held):
    _, _, z, _ = grid_place()
    got = swap_ctx(pick(held, 1 - z // 2, 0), Z_FAR)
    return pick(held, z // 2, 0).astype(jnp.float32) + got.astype(jnp.float32)


def norm_parts(rows):
    width = rows.shape[-1]
    totals = jnp.sum(rows, axis=-1, keepdims=True)
    meansq = (jnp.sum(rows * rows, axis=-1, keepdims=True) + totals * totals) / width
    scale = lax.rsqrt(meansq + EPS)
    last = lax.broadcasted_iota(jnp.int32, rows.shape, 1) == width - 1
    return jnp.where(last, -totals, rows) * scale, scale


def norm_back(normed, scale, gains, grads):
    width = normed.shape[-1]
    weighted = grads * gains
    mean = jnp.sum(weighted * normed, axis=-1, keepdims=True) / width
    grad_u = scale * (weighted - normed * mean)
    last = lax.broadcasted_iota(jnp.int32, grad_u.shape, 1) == width - 1
    final = jnp.sum(jnp.where(last, grad_u, 0.0), axis=-1, keepdims=True)
    return jnp.where(last, 0.0, grad_u - final)


def stack_heads(block):
    head = lax.broadcasted_iota(jnp.int32, block.shape, 1) // HEAD_DIM
    return jnp.concatenate([jnp.where(head == i, block, jnp.zeros_like(block)) for i in range(4)], axis=0)


def unstack_heads(turned):
    rows = turned.T
    head = lax.broadcasted_iota(jnp.int32, (LOCAL, 4 * HEAD_DIM), 1) // HEAD_DIM
    picked = rows[:LOCAL]
    for i in range(1, 4):
        picked = jnp.where(head == i, rows[i * LOCAL : (i + 1) * LOCAL], picked)
    return picked


def attend_kernel(starts, q_ref, k_ref, v_ref, key_ref, query_ref, out_ref, probs_ref, bias_ref):
    window = pl.ds(pl.multiple_of(starts[pl.program_id(0)], 32), WINDOW)

    @pl.when(pl.program_id(1) == 0)
    def _():
        same = key_ref[window, 0:1] == query_ref[0, 0:1, :]
        causal = key_ref[window, 1:2] <= query_ref[0, 1:2, :]
        bias_ref[...] = jnp.where(same & causal, 0.0, NEG)

    stacked = stack_heads(q_ref[...])
    scores = matmul_right_t(k_ref[window, :], stacked) + bias_ref[...]
    weights = jnp.exp(scores - jnp.max(scores, axis=0, keepdims=True))
    probs = (weights * (1.0 / jnp.sum(weights, axis=0, keepdims=True))).astype(jnp.bfloat16)
    probs_ref[0, 0] = probs
    out_ref[...] = unstack_heads(matmul(v_ref[window, :].T, probs)).astype(jnp.bfloat16)


def attend(queries, keys, values, starts, key_marks, query_marks):
    return pl.pallas_call(
        attend_kernel,
        grid_spec=pltpu.PrefetchScalarGridSpec(
            num_scalar_prefetch=1,
            grid=(3, 3),
            in_specs=[
                pl.BlockSpec((LOCAL, 256), lambda j, h, s: (j, h)),
                pl.BlockSpec((KEYS, 256), lambda j, h, s: (0, h)),
                pl.BlockSpec((KEYS, 256), lambda j, h, s: (0, h)),
                pl.BlockSpec((KEYS, 2), lambda j, h, s: (0, 0)),
                pl.BlockSpec((1, 2, 4 * LOCAL), lambda j, h, s: (j, 0, 0)),
            ],
            out_specs=[
                pl.BlockSpec((LOCAL, 256), lambda j, h, s: (j, h)),
                pl.BlockSpec((1, 1, WINDOW, 4 * LOCAL), lambda j, h, s: (j, h, 0, 0)),
            ],
            scratch_shapes=[pltpu.VMEM((WINDOW, 4 * LOCAL), jnp.float32)],
        ),
        out_shape=[
            jax.ShapeDtypeStruct((ROWS, 768), jnp.bfloat16),
            jax.ShapeDtypeStruct((3, 3, WINDOW, 4 * LOCAL), jnp.bfloat16),
        ],
        compiler_params=pltpu.CompilerParams(vmem_limit_bytes=40 * 1024 * 1024),
        cost_estimate=pl.CostEstimate(flops=3_000_000_000, bytes_accessed=12_000_000, transcendentals=2_700_000),
        name="attend",
    )(starts, queries, keys, values, key_marks, query_marks)


def attend_back_kernel(
    starts, q_ref, k_ref, v_ref, grad_ref, probs_ref, grad_q_ref, grad_k_ref, grad_v_ref, sum_k, sum_v
):
    row_block = pl.program_id(1)
    window = pl.ds(pl.multiple_of(starts[row_block], 32), WINDOW)

    @pl.when(row_block == 0)
    def _():
        sum_k[...] = jnp.zeros_like(sum_k)
        sum_v[...] = jnp.zeros_like(sum_v)

    probs = probs_ref[0, 0]
    grads = stack_heads(grad_ref[...])
    wide = probs.astype(jnp.float32)
    terms = wide * matmul_right_t(v_ref[window, :], grads)
    grad_scores = (terms - wide * jnp.sum(terms, axis=0, keepdims=True)).astype(jnp.bfloat16)
    sum_v[window, :] += matmul(probs, grads)
    sum_k[window, :] += matmul(grad_scores, stack_heads(q_ref[...]))
    grad_q = unstack_heads(matmul(k_ref[window, :].T, grad_scores)) * SCALE
    grad_q_ref[...] = grad_q.astype(jnp.bfloat16)

    @pl.when(row_block == 2)
    def _():
        grad_k_ref[...] = sum_k[...].astype(jnp.bfloat16)
        grad_v_ref[...] = sum_v[...].astype(jnp.bfloat16)


def attend_back(queries, keys, values, grads, probs, starts):
    return pl.pallas_call(
        attend_back_kernel,
        grid_spec=pltpu.PrefetchScalarGridSpec(
            num_scalar_prefetch=1,
            grid=(3, 3),
            in_specs=[
                pl.BlockSpec((LOCAL, 256), lambda h, j, s: (j, h)),
                pl.BlockSpec((KEYS, 256), lambda h, j, s: (0, h)),
                pl.BlockSpec((KEYS, 256), lambda h, j, s: (0, h)),
                pl.BlockSpec((LOCAL, 256), lambda h, j, s: (j, h)),
                pl.BlockSpec((1, 1, WINDOW, 4 * LOCAL), lambda h, j, s: (j, h, 0, 0)),
            ],
            out_specs=[
                pl.BlockSpec((LOCAL, 256), lambda h, j, s: (j, h)),
                pl.BlockSpec((KEYS, 256), lambda h, j, s: (0, h)),
                pl.BlockSpec((KEYS, 256), lambda h, j, s: (0, h)),
            ],
            scratch_shapes=[pltpu.VMEM((KEYS, 256), jnp.float32), pltpu.VMEM((KEYS, 256), jnp.float32)],
        ),
        out_shape=[
            jax.ShapeDtypeStruct((ROWS, 768), jnp.bfloat16),
            jax.ShapeDtypeStruct((KEYS, 768), jnp.bfloat16),
            jax.ShapeDtypeStruct((KEYS, 768), jnp.bfloat16),
        ],
        compiler_params=pltpu.CompilerParams(vmem_limit_bytes=40 * 1024 * 1024),
        cost_estimate=pl.CostEstimate(flops=7_000_000_000, bytes_accessed=14_000_000, transcendentals=0),
        name="attend_back",
    )(starts, queries, keys, values, grads, probs)


def widen(array):
    return jnp.pad(array, [(0, 0)] * (array.ndim - 1) + [(0, 1)])


def send_home(delta):
    delta = delta.reshape(3, -1, delta.shape[-1])
    return [swap_ctx(delta[j], RETURN[j]) for j in range(3)]


def at_home(parts, base, ctx):
    home = jnp.zeros((3,) + parts[0].shape, parts[0].dtype)
    for j, part in enumerate(parts):
        home = lax.dynamic_update_index_in_dim(home, part, (2 * j + ctx) % 3, 0)
    return base.astype(jnp.float32) + home[..., : base.shape[-1]].astype(jnp.float32)


def spread_body(
    tokens,
    segment_ids,
    qkv_weight,
    out_weight,
    up_weight,
    down_weight,
    attn_gain,
    mlp_gain,
    out_cotangent,
):
    micro_count, _, local_len, res_width = tokens.shape
    width = res_width + 1
    ctx = lax.axis_index("ctx")
    tokens = tokens.reshape(micro_count, local_len, res_width)
    cotangent = out_cotangent.reshape(micro_count, local_len, res_width)

    gains_own = jnp.pad(jnp.stack([attn_gain, mlp_gain], axis=1), ((0, 0), (0, 126)))
    rows_own, ff = up_weight.shape
    def deal(array):
        return [swap_ctx(pick(array, (2 * j + ctx) % 3, 0), DEAL[j]) for j in range(3)]

    def meet(flag, *values):
        return lax.optimization_barrier(values) if FLAGS[flag] else values

    wide, cotangent_wide = widen(tokens), widen(cotangent)
    if FLAGS["deal"] == 1:
        both = deal(jnp.concatenate([wide, cotangent_wide], axis=1))
        dealt = [part[:local_len] for part in both]
        grad_rows = [part[local_len:] for part in both]
    else:
        dealt, grad_rows = deal(wide), []
    far = swap_ctx(wide[1], [(0, 5)])
    early_own = jnp.concatenate([qkv_weight, gains_own], axis=1)
    early_cut = FLAGS["cut"]
    up_own, down_own = jnp.concatenate([widen(out_weight), up_weight], axis=1), widen(down_weight)
    pair = jnp.stack([early_own, swap_ctx(early_own, Z_FAR)])
    pair, up_own, down_own = meet("f0", pair, up_own, down_own)
    line = jnp.stack([pair, swap_ctx(pair, Z_SWAP)])
    dealt, far, line, up_own, down_own, cotangent_wide, grad_rows = meet(
        "f1", dealt, far, line, up_own, down_own, cotangent_wide, grad_rows
    )
    inputs_low = jnp.concatenate(dealt, axis=0)
    near = plane_start(line, early_cut)
    up_own = after(up_own, line)
    up_pair = jnp.stack([up_own, swap_ctx(up_own, Z_FAR)])
    if FLAGS["deal"] == 0:
        grad_rows = [swap_ctx(pick(cotangent_wide, (2 * j + ctx) % 3, 0), DEAL[j]) for j in range(2)]
    near, up_pair, inputs_low = meet("f2", near, up_pair, inputs_low)
    ends = plane_end(*near)
    up_line = jnp.stack([up_pair, swap_ctx(up_pair, Z_SWAP)])
    if FLAGS["deal"] == 0:
        grad_rows.append(swap_ctx(pick(cotangent_wide, (4 + ctx) % 3, 0), DEAL[2]))
    up_line, ends, inputs_low, grad_rows = meet("f3", up_line, ends, inputs_low, grad_rows)
    pieces = [*near, *ends]
    others = other_core(pieces)
    up_near = plane_start(up_line, (width + ff) // 2)
    down_own = after(down_own, up_line)
    down_pair = jnp.stack([down_own, swap_ctx(down_own, Z_FAR)])
    below = [None, None]
    if FLAGS["shift"] in (0, 1):
        below[0] = swap_ctx(inputs_low, UP[0])
    if FLAGS["shift"] == 0:
        below[1] = swap_ctx(inputs_low, UP[1])
    up_near, down_pair, others, below, inputs_low, cotangent_wide = meet(
        "f4", up_near, down_pair, others, below, inputs_low, cotangent_wide
    )
    (first,) = all_rows(pieces, others, early_own.shape[1], 0, early_cut, width)
    up_ends = plane_end(*up_near)
    down_line = jnp.stack([down_pair, swap_ctx(down_pair, Z_SWAP)])
    if FLAGS["shift"] == 2:
        below[0] = swap_ctx(inputs_low, UP[0])
    if FLAGS["shift"] in (1, 2):
        below[1] = swap_ctx(inputs_low, UP[1])
    down_line, up_ends, below, _ = meet("f5", down_line, up_ends, below, first)
    if FLAGS["deal"] == 3:
        grad_rows = deal(cotangent_wide)
    down_near = plane_start(down_line, width // 2)
    up_others = other_core([*up_near, *up_ends])
    key_rows = jnp.concatenate([far, below[1], below[0], inputs_low], axis=0).astype(jnp.float32)
    q_full, second = first[:, :width], first[:, width : 3 * width]
    gain_one = first[:, 3 * width].astype(jnp.float32)
    gain_two = first[:, 3 * width + 1].astype(jnp.float32)

    ids = segment_ids.reshape(micro_count, -1) + 8 * jnp.arange(micro_count, dtype=jnp.int32)[:, None]
    ids = jnp.concatenate([jnp.full((KEYS - ROWS,), -1, jnp.int32), ids.reshape(-1)])
    ids = lax.dynamic_slice_in_dim(ids, ROWS * ctx, KEYS, 0)
    places = jnp.arange(KEYS, dtype=jnp.int32)
    key_marks = jnp.stack([ids, places], axis=1)
    query_marks = jnp.stack([ids, places])[:, KEYS - ROWS :].reshape(2, 3, local_len)
    query_marks = jnp.tile(jnp.moveaxis(query_marks, 0, 1), (1, 1, 4))
    flat = 3 * ctx + jnp.arange(3, dtype=jnp.int32)
    starts = jnp.clip(8 * (flat // 8) + 7 - 3 * ctx, 0, 2) * local_len

    inputs = key_rows[KEYS - ROWS :]
    key_normed, key_scale = norm_parts(key_rows)
    norm_keys = (key_normed * gain_one).astype(jnp.bfloat16)
    norm_a = norm_keys[KEYS - ROWS :]
    queries = (matmul(norm_a, q_full).astype(jnp.bfloat16) * SCALE).astype(jnp.bfloat16)
    keys_values = matmul(norm_keys, second).astype(jnp.bfloat16)
    keys, values = keys_values[:, :width], keys_values[:, width:]
    queries, keys, values, down_near, up_others = meet("f6", queries, keys, values, down_near, up_others)
    down_ends = plane_end(*down_near)
    if FLAGS["deal"] == 2:
        grad_rows = deal(cotangent_wide)
    attn, probs = attend(queries, keys, values, starts, key_marks, query_marks)
    attn, down_ends, up_others, grad_rows = meet("f7", attn, down_ends, up_others, grad_rows)
    grad_rows = jnp.concatenate(grad_rows, axis=0)
    down_pieces = [*down_near, *down_ends]
    down_others = other_core(down_pieces)
    (out_up_full,) = all_rows([*up_near, *up_ends], up_others, width + ff, 0, (width + ff) // 2, width)
    out_full, up_full = out_up_full[:, :width], out_up_full[:, width:]
    branch = matmul(attn, out_full)
    mixed = inputs + branch
    mixed_normed, mixed_scale = norm_parts(mixed)
    norm_m, down_others = meet("f8", (mixed_normed * gain_two).astype(jnp.bfloat16), down_others)
    (down_full,) = all_rows(down_pieces, down_others, width, 0, width // 2, width)
    pre = matmul(norm_m, up_full)
    act, gelu_pull = jax.vjp(gelu_tanh, pre)
    act = act.astype(jnp.bfloat16)

    if FLAGS["dfold"]:
        down_got = fold_send(act, grad_rows)
    else:
        grad_down = matmul_left_t(act, grad_rows).astype(jnp.bfloat16)
        grad_rows = after(grad_rows, grad_down)
        down_got = fold_part(grad_down)
    grad_pre = gelu_pull(matmul_right_t(grad_rows, down_full))[0].astype(jnp.bfloat16)
    result_delta = (branch + matmul(act, down_full)).astype(jnp.bfloat16)
    deltas = result_delta.reshape(3, local_len, width)
    home = []
    if FLAGS["home"] == 1:
        home = send_home(result_delta)
    down_got, grad_pre = meet("b0", down_got, grad_pre)
    down_near = fold_start(*halves(fold_core(act, grad_rows, down_got) if FLAGS["dfold"] else down_got))
    if FLAGS["ufold"]:
        up_got = fold_send(norm_m, grad_pre)
    else:
        grad_up = matmul_left_t(norm_m, grad_pre).astype(jnp.bfloat16)
        up_held = fold_part(grad_up)
        if FLAGS["upfirst"]:
            grad_pre = after(grad_pre, grad_up)
    grad_norm_m = matmul_right_t(grad_pre, up_full)
    grad_gain_two = jnp.sum(grad_norm_m * mixed_normed, axis=0)
    grad_mixed_norm = norm_back(mixed_normed, mixed_scale, gain_two, grad_norm_m)
    grad_branch = (grad_rows.astype(jnp.float32) + grad_mixed_norm).astype(jnp.bfloat16)
    grad_attn = matmul_right_t(grad_branch, out_full).astype(jnp.bfloat16)
    if FLAGS["ufold"]:
        up_held = fold_core(norm_m, grad_pre, up_got)
    if FLAGS["outin"]:
        grad_out = matmul_left_t(attn, grad_branch).astype(jnp.bfloat16)
        grad_attn, grad_out = meet("b1", grad_attn, grad_out)
    grad_attn, grad_branch, down_near, up_held, home, deltas = meet(
        "b2", grad_attn, grad_branch, down_near, up_held, home, deltas
    )
    down_line, up_near = fold_end(*down_near), fold_start(*halves(up_held))
    if FLAGS["home"] == 2:
        home = [swap_ctx(deltas[0], RETURN[0])]
    grad_q, grad_k, grad_v = attend_back(queries, keys, values, grad_attn, probs, starts)
    grad_q, grad_k, grad_v, down_line, up_near, home, deltas = meet(
        "b3", grad_q, grad_k, grad_v, down_line, up_near, home, deltas
    )
    if FLAGS["home"] == 2:
        home = home + [swap_ctx(deltas[j], RETURN[j]) for j in (1, 2)]
    up_line = fold_end(*up_near)
    if FLAGS["dz"]:
        down_pair = fold_near_z(down_line)
    grad_kv = jnp.concatenate([grad_k, grad_v], axis=1)
    grad_norm_keys = matmul_right_t(grad_kv, second)
    grad_below = grad_norm_keys[: KEYS - ROWS].astype(jnp.bfloat16)
    sent = [grad_below[4 * local_len :], grad_below[local_len : 4 * local_len], grad_below[:local_len]]
    back = []
    for part, pairs in zip(sent, UP):
        if FLAGS["c"] and len(back) == 2:
            part = after(part, back)
        back.append(swap_ctx(part, [(high, low) for low, high in pairs]))
    if FLAGS["dxfirst"]:
        grad_kv, grad_q = after((grad_kv, grad_q), grad_below)
    grad_norm_q = matmul_right_t(grad_q, q_full)
    grad_gain_one = jnp.sum(grad_norm_keys * key_normed, axis=0)
    grad_gain_one = grad_gain_one + jnp.sum(grad_norm_q * key_normed[KEYS - ROWS :], axis=0)
    gains = jnp.pad(jnp.stack([grad_gain_one, grad_gain_two], axis=1).astype(jnp.bfloat16), ((0, 0), (0, 126)))
    _, core, _, _ = grid_place()
    grad_q_weight = matmul_left_t(norm_a, grad_q).astype(jnp.bfloat16)
    grad_kv_weight = matmul_left_t(norm_keys, grad_kv).astype(jnp.bfloat16)
    if not FLAGS["outin"]:
        grad_out = matmul_left_t(attn, grad_branch).astype(jnp.bfloat16)
    early_parts = [part.reshape(2, 2, 8 * rows_own, -1) for part in (grad_q_weight, grad_kv_weight, grad_out, gains)]
    early_got = swap_seq(jnp.concatenate([pick(part, 1 - core, 1) for part in early_parts], axis=-1), CORE_SWAP)
    early_held = add_low(jnp.concatenate([pick(part, core, 1) for part in early_parts], axis=-1), early_got)
    early_held, up_line = meet("b4", early_held, up_line)
    if FLAGS["home"] != 0:
        home, up_line = meet("b5", home, up_line)
        result = at_home(home, tokens, ctx)
    early_held = early_held.reshape(2, 4, 2, rows_own, -1)
    early_left, early_right = early_held[..., : 2 * width], early_held[..., 2 * width :]
    early_near = fold_start(early_left, early_right)
    if not FLAGS["dz"]:
        up_line = jnp.concatenate(
            [up_line] + [down_line[:, i * rows_own : (i + 1) * rows_own] for i in range(4)], axis=2
        )
    if FLAGS["lz"] == 0:
        up_pair = fold_near_z(up_line)
        early_near, back, up_pair = meet("b6", early_near, back, up_pair)
    else:
        early_near, back, up_line = meet("b6", early_near, back, up_line)
        up_pair = fold_near_z(up_line)
    early_line = fold_end(*early_near)
    early_line, up_pair = meet("b7", early_line, up_pair)
    grad_norm_a = grad_norm_keys[KEYS - ROWS :] + grad_norm_q + back[0].astype(jnp.float32) + back[1].astype(jnp.float32)
    grad_norm_a = grad_norm_a + jnp.pad(back[2].astype(jnp.float32), ((2 * local_len, 0), (0, 0)))
    grad_input_norm = norm_back(
        key_normed[KEYS - ROWS :], key_scale[KEYS - ROWS :], gain_one, grad_norm_a
    )
    grad_delta = (grad_mixed_norm + grad_input_norm).astype(jnp.bfloat16)
    if FLAGS["ez"]:
        early_sum = fold_far_z(fold_near_z(early_line))
    else:
        early_sum = fold_z(early_line)
    if FLAGS["home"] == 0:
        deltas = jnp.stack([deltas, grad_delta.reshape(3, local_len, width)], axis=1)
        parts = send_home(deltas)
        result = at_home([part[:local_len] for part in parts], tokens, ctx)
        grad_tokens = at_home([part[local_len:] for part in parts], cotangent, ctx)
    else:
        grad_tokens = at_home(send_home(grad_delta), cotangent, ctx)
    late_sum = fold_far_z(up_pair)
    grad_up = late_sum[:, :ff]
    if FLAGS["dz"]:
        grad_down = fold_far_z(down_pair)
    else:
        grad_down = jnp.concatenate([late_sum[:, ff + i * width : ff + (i + 1) * width] for i in range(4)], axis=0)
    grad_qkv, grad_out = early_sum[:, : 3 * width], early_sum[:, 3 * width : 4 * width]
    grad_gain_one, grad_gain_two = early_sum[:, 4 * width], early_sum[:, 4 * width + 1]
    shape = (micro_count, 1, local_len, res_width)
    return (
        result.reshape(shape),
        grad_tokens.reshape(shape),
        grad_qkv,
        grad_out[:, :res_width],
        grad_up,
        grad_down[:, :res_width],
        grad_gain_one,
        grad_gain_two,
    )


def solution(mesh):
    small = (mesh.shape["seq"], mesh.shape["ctx"]) == (4, 8)
    return jax.shard_map(
        spread_body if small else body,
        mesh=mesh,
        in_specs=(
            P(None, "seq", "ctx", None),
            P(None, "seq", None),
            P(("seq", "ctx"), None),
            P(("seq", "ctx"), None),
            P(("seq", "ctx"), None),
            P(("seq", "ctx"), None),
            P(("seq", "ctx")),
            P(("seq", "ctx")),
            P(None, "seq", "ctx", None),
        ),
        out_specs=(
            P(None, "seq", "ctx", None),
            P(None, "seq", "ctx", None),
            P(("seq", "ctx"), None),
            P(("seq", "ctx"), None),
            P(("seq", "ctx"), None),
            P(("seq", "ctx"), None),
            P(("seq", "ctx")),
            P(("seq", "ctx")),
        ),
        check_vma=False,
    )
```

```python
import functools
import math

import jax
import jax.numpy as jnp
import numpy as np
from jax import lax
from jax.experimental import pallas as pl
from jax.experimental.pallas import tpu as pltpu
from jax.sharding import PartitionSpec as P

HEADS = 12
HEAD_DIM = 64


EPS = 1e-05
NEG = -1e30
SCALE = 0.125


def crms(inputs, gains):
    totals = jnp.sum(inputs, axis=-1, keepdims=True)
    meansq = (jnp.sum(inputs * inputs, axis=-1, keepdims=True) + totals * totals) / gains.shape[0]
    return jnp.concatenate([inputs, -totals], axis=-1) * lax.rsqrt(meansq + EPS) * gains


def gelu_tanh(inputs):
    return jax.nn.gelu(inputs, approximate=True)


def matmul(left, right):
    return jnp.dot(left, right, preferred_element_type=jnp.float32)


def matmul_left_t(left, right):
    return lax.dot_general(
        left, right, (((0,), (0,)), ((), ())), preferred_element_type=jnp.float32
    )


def matmul_right_t(left, right):
    return lax.dot_general(
        left, right, (((1,), (1,)), ((), ())), preferred_element_type=jnp.float32
    )


def allowed_pairs(query_pos, query_seg, key_pos, key_seg):
    same_doc = query_seg[:, None, :, None] == key_seg[:, None, None, :]
    causal = query_pos[None, None, :, None] >= key_pos[None, None, None, :]
    return same_doc & causal


def attend_block(state, queries, query_pos, query_seg, keys, values, key_pos, key_seg):
    best, denom, accum = state
    scores = (
        jnp.einsum("bqhd,bkhd->bhqk", queries, keys, preferred_element_type=jnp.float32) * SCALE
    )
    allowed = allowed_pairs(query_pos, query_seg, key_pos, key_seg)
    scores = jnp.where(allowed, scores, NEG)
    peak = jnp.maximum(best, jnp.max(scores, axis=-1))
    weights = jnp.where(allowed, jnp.exp(scores - peak[..., None]), 0.0)
    factor = jnp.exp(best - peak)
    denom = denom * factor + jnp.sum(weights, axis=-1)
    accum = accum * factor[..., None] + jnp.einsum(
        "bhqk,bkhd->bhqd", weights.astype(jnp.bfloat16), values, preferred_element_type=jnp.float32
    )
    return (peak, denom, accum)


def pair_grads(queries, grad_o, lse, delta, query_pos, query_seg, keys, values, key_pos, key_seg):
    scores = (
        jnp.einsum("bqhd,bkhd->bhqk", queries, keys, preferred_element_type=jnp.float32) * SCALE
    )
    allowed = allowed_pairs(query_pos, query_seg, key_pos, key_seg)
    probs = jnp.where(allowed, jnp.exp(scores - lse[..., None]), 0.0)
    dprobs = jnp.einsum("bqhd,bkhd->bhqk", grad_o, values, preferred_element_type=jnp.float32)
    grad_scores = (probs * (dprobs - delta[..., None])).astype(jnp.bfloat16)
    part_q = (
        jnp.einsum("bhqk,bkhd->bqhd", grad_scores, keys, preferred_element_type=jnp.float32) * SCALE
    )
    part_k = (
        jnp.einsum("bhqk,bqhd->bkhd", grad_scores, queries, preferred_element_type=jnp.float32)
        * SCALE
    )
    part_v = jnp.einsum(
        "bhqk,bqhd->bkhd", probs.astype(jnp.bfloat16), grad_o, preferred_element_type=jnp.float32
    )
    return (part_q, part_k, part_v)


def body(
    tokens,
    segment_ids,
    qkv_weight,
    out_weight,
    up_weight,
    down_weight,
    attn_gain,
    mlp_gain,
    out_cotangent,
):
    micro_count, seq_count, local_len, res_width = tokens.shape
    length = segment_ids.shape[2]
    first = lax.axis_index("ctx") * local_len
    query_pos = first + jnp.arange(local_len, dtype=jnp.int32)
    row_count = seq_count * local_len

    def fetch():
        return (
            lax.all_gather(qkv_weight, ("seq", "ctx"), axis=0, tiled=True),
            lax.all_gather(out_weight, ("seq", "ctx"), axis=0, tiled=True),
            lax.all_gather(up_weight, ("seq", "ctx"), axis=0, tiled=True),
            lax.all_gather(down_weight, ("seq", "ctx"), axis=0, tiled=True),
            lax.all_gather(attn_gain, ("seq", "ctx"), axis=0, tiled=True),
            lax.all_gather(mlp_gain, ("seq", "ctx"), axis=0, tiled=True),
        )

    def backward(number, gathered, saved):
        qkv_full, out_full, up_full, down_full, gain_one, gain_two = gathered
        (
            inputs,
            seg_rows,
            query_seg,
            norm_a,
            queries,
            keys_own,
            values_own,
            attn_f32,
            lse,
            attn,
            mixed,
            norm_m,
            pre,
            act,
        ) = saved
        width = qkv_full.shape[0]
        grad_y = out_cotangent[number].reshape(row_count, res_width)
        grad_down = matmul_left_t(act, grad_y)
        grad_act = matmul_right_t(grad_y, down_full)
        _, gelu_pull = jax.vjp(gelu_tanh, pre)
        grad_pre = gelu_pull(grad_act)[0].astype(jnp.bfloat16)
        grad_up = matmul_left_t(norm_m, grad_pre)
        grad_norm_m = matmul_right_t(grad_pre, up_full)
        _, pull_two = jax.vjp(crms, mixed, gain_two.astype(jnp.float32))
        grad_mixed_norm, grad_gain_two = pull_two(grad_norm_m)
        grad_mixed = grad_y.astype(jnp.float32) + grad_mixed_norm
        grad_branch = grad_mixed.astype(jnp.bfloat16)
        grad_outw = matmul_left_t(attn, grad_branch)
        grad_attn = (
            matmul_right_t(grad_branch, out_full)
            .astype(jnp.bfloat16)
            .reshape(seq_count, local_len, HEADS, HEAD_DIM)
        )
        delta = jnp.transpose(jnp.sum(grad_attn.astype(jnp.float32) * attn_f32, axis=-1), (0, 2, 1))
        block_len = math.gcd(length, 1024)
        block_ids = jnp.arange(length // block_len, dtype=jnp.int32)
        keys_all, values_all = (
            lax.all_gather(keys_own, "ctx", axis=1, tiled=True),
            lax.all_gather(values_own, "ctx", axis=1, tiled=True),
        )

        def back_keys(carry, number_block):
            offset = number_block * block_len
            key_block = lax.dynamic_slice_in_dim(keys_all, offset, block_len, 1)
            value_block = lax.dynamic_slice_in_dim(values_all, offset, block_len, 1)
            key_pos = offset + jnp.arange(block_len, dtype=jnp.int32)
            key_seg = lax.dynamic_slice_in_dim(seg_rows, offset, block_len, 1)
            part_q, part_k, part_v = pair_grads(
                queries,
                grad_attn,
                lse,
                delta,
                query_pos,
                query_seg,
                key_block,
                value_block,
                key_pos,
                key_seg,
            )
            return (carry + part_q, jnp.concatenate([part_k, part_v], axis=-1))

        grad_q, terms = lax.scan(back_keys, jnp.zeros(queries.shape, jnp.float32), block_ids)
        terms = jnp.moveaxis(terms, 0, 1).reshape(seq_count, length, HEADS, 2 * HEAD_DIM)
        owned_terms = lax.psum_scatter(terms, "ctx", scatter_dimension=1, tiled=True)
        grad_k = owned_terms[..., :HEAD_DIM]
        grad_v = owned_terms[..., HEAD_DIM:]
        grad_qkv = jnp.concatenate(
            [
                grad_q.reshape(row_count, width),
                grad_k.reshape(row_count, width),
                grad_v.reshape(row_count, width),
            ],
            axis=-1,
        ).astype(jnp.bfloat16)
        grad_qkvw = matmul_left_t(norm_a, grad_qkv)
        grad_norm_a = matmul_right_t(grad_qkv, qkv_full)
        _, pull_one = jax.vjp(crms, inputs, gain_one.astype(jnp.float32))
        grad_input_norm, grad_gain_one = pull_one(grad_norm_a)
        grad_inputs = (grad_mixed + grad_input_norm).reshape(seq_count, local_len, res_width)
        return (
            grad_inputs,
            (grad_qkvw, grad_outw, grad_up, grad_down, grad_gain_one, grad_gain_two),
        )

    outputs = []
    input_grads = []
    owned = None
    for number in range(micro_count):
        (
            forward_qkv_full,
            forward_out_full,
            forward_up_full,
            forward_down_full,
            forward_gain_one,
            forward_gain_two,
        ) = fetch()
        forward_width = forward_qkv_full.shape[0]
        forward_inputs = tokens[number].astype(jnp.float32).reshape(row_count, res_width)
        forward_seg_rows = segment_ids[number]
        forward_query_seg = lax.dynamic_slice_in_dim(forward_seg_rows, first, local_len, 1)
        forward_norm_a = crms(forward_inputs, forward_gain_one.astype(jnp.float32)).astype(
            jnp.bfloat16
        )
        qkv = matmul(forward_norm_a, forward_qkv_full).astype(jnp.bfloat16)
        forward_queries = qkv[:, :forward_width].reshape(seq_count, local_len, HEADS, HEAD_DIM)
        forward_keys_own = qkv[:, forward_width : 2 * forward_width].reshape(
            seq_count, local_len, HEADS, HEAD_DIM
        )
        forward_values_own = qkv[:, 2 * forward_width :].reshape(
            seq_count, local_len, HEADS, HEAD_DIM
        )

        def fold_keys(state, piece):
            keys_part, values_part = piece
            span = keys_part.shape[1]
            block_len = span if span <= 1024 else math.gcd(span, 1024)

            def inner(carry, number_block):
                offset = number_block * block_len
                key_block = lax.dynamic_slice_in_dim(keys_part, offset, block_len, 1)
                value_block = lax.dynamic_slice_in_dim(values_part, offset, block_len, 1)
                key_pos = offset + jnp.arange(block_len, dtype=jnp.int32)
                key_seg = lax.dynamic_slice_in_dim(forward_seg_rows, offset, block_len, 1)
                return (
                    attend_block(
                        carry,
                        forward_queries,
                        query_pos,
                        forward_query_seg,
                        key_block,
                        value_block,
                        key_pos,
                        key_seg,
                    ),
                    None,
                )

            state, _ = lax.scan(inner, state, jnp.arange(span // block_len, dtype=jnp.int32))
            return state

        initial = (
            jnp.full((seq_count, HEADS, local_len), NEG, jnp.float32),
            jnp.zeros((seq_count, HEADS, local_len), jnp.float32),
            jnp.zeros((seq_count, HEADS, local_len, HEAD_DIM), jnp.float32),
        )
        best, denom, accum = fold_keys(
            initial,
            (
                lax.all_gather(forward_keys_own, "ctx", axis=1, tiled=True),
                lax.all_gather(forward_values_own, "ctx", axis=1, tiled=True),
            ),
        )
        heads_out = accum / denom[..., None]
        forward_lse = best + jnp.log(denom)
        forward_attn_f32 = jnp.transpose(heads_out, (0, 2, 1, 3))
        forward_attn = forward_attn_f32.reshape(row_count, forward_width).astype(jnp.bfloat16)
        forward_mixed = forward_inputs + matmul(forward_attn, forward_out_full)
        forward_norm_m = crms(forward_mixed, forward_gain_two.astype(jnp.float32)).astype(
            jnp.bfloat16
        )
        forward_pre = matmul(forward_norm_m, forward_up_full)
        forward_act = gelu_tanh(forward_pre).astype(jnp.bfloat16)
        result = (forward_mixed + matmul(forward_act, forward_down_full)).reshape(
            seq_count, local_len, res_width
        )
        forward_saved = (
            forward_inputs,
            forward_seg_rows,
            forward_query_seg,
            forward_norm_a,
            forward_queries,
            forward_keys_own,
            forward_values_own,
            forward_attn_f32,
            forward_lse,
            forward_attn,
            forward_mixed,
            forward_norm_m,
            forward_pre,
            forward_act,
        )
        result, saved = (result, forward_saved)
        grad_inputs, grads = backward(number, fetch(), saved)
        outputs.append(result)
        input_grads.append(grad_inputs)
        shares = (
            lax.psum_scatter(grads[0], ("seq", "ctx"), scatter_dimension=0, tiled=True),
            lax.psum_scatter(grads[1], ("seq", "ctx"), scatter_dimension=0, tiled=True),
            lax.psum_scatter(grads[2], ("seq", "ctx"), scatter_dimension=0, tiled=True),
            lax.psum_scatter(grads[3], ("seq", "ctx"), scatter_dimension=0, tiled=True),
            lax.psum_scatter(grads[4], ("seq", "ctx"), scatter_dimension=0, tiled=True),
            lax.psum_scatter(grads[5], ("seq", "ctx"), scatter_dimension=0, tiled=True),
        )
        owned = shares if owned is None else jax.tree.map(jnp.add, owned, shares)
    return (jnp.stack(outputs), jnp.stack(input_grads)) + tuple(owned)


FLAGS = {'deal': 3, 'cut': 1280, 'shift': 1, 'f0': 0, 'f1': 1, 'f2': 1, 'f3': 1, 'f4': 0, 'f5': 1, 'f6': 1, 'f7': 0, 'f8': 2, 'home': 0, 'b0': 1, 'b1': 0, 'b2': 1, 'b3': 1, 'b4': 2, 'b5': 0, 'b6': 1, 'b7': 0, 'outin': 1, 'dz': 0, 'c': 1, 'dxfirst': 1, 'lz': 0, 'ez': 1, 'dfold': 0, 'ufold': 0, 'upfirst': 1, 'kvg': 1, 'u2': 1, 'homeg': 2, 'lz2g': 1, 'ab': 1, 'dfar': 0, 'late_result': 1, 'any': 0}
SLOTS = 10
LOCAL = 96
WINDOW = 768
ROWS = 3 * LOCAL
KEYS = SLOTS * LOCAL
Z_SWAP = [(i, i ^ 2) for i in range(8)]
Z_FAR = [(i, i ^ 4) for i in range(8)]
Z_SHIFT = [[(i, (i + 2 * k) % 8) for i in range(8)] for k in range(4)]
Y_SWAP = [(i, i ^ 1) for i in range(8)]
X_SWAP = [(i, i ^ 2) for i in range(4)]
CORE_SWAP = [(i, i ^ 1) for i in range(4)]
DEAL = [[(f % 8, f // 3) for f in range(24) if f % 3 == j] for j in range(3)]
RETURN = [[(f // 3, f % 8) for f in range(24) if f % 3 == j] for j in range(3)]
UP = ([(d, d + 1) for d in range(7)], [(0, 2), (2, 4), (3, 5), (5, 7)], [(2, 5)])


def swap_seq(array, pairs):
    return lax.ppermute(array, "seq", pairs)


def swap_ctx(array, pairs):
    return lax.ppermute(array, "ctx", pairs)


def after(value, *others):
    return lax.optimization_barrier((value, others))[0]


def grid_place():
    seq, ctx = lax.axis_index("seq"), lax.axis_index("ctx")
    return seq // 2, seq % 2, ctx // 2, ctx % 2


def along_z(own, *others):
    pair = jnp.stack([own, swap_ctx(own, Z_FAR)])
    return jnp.stack([pair, swap_ctx(after(pair, *others), Z_SWAP)])


def plane_start(line, split):
    left, right = line[..., :split], line[..., split:]
    return jnp.stack([left, swap_seq(left, X_SWAP)]), jnp.stack([right, swap_ctx(right, Y_SWAP)])


def plane_end(left, right):
    return swap_ctx(left, Y_SWAP), swap_seq(right, X_SWAP)


def other_core(pieces):
    return [swap_seq(piece, CORE_SWAP) for piece in pieces]


def place_kernel(cuts, *refs):
    pieces, out_refs, sems = refs[:8], refs[8:-1], refs[-1]
    x, core, z, y = grid_place()
    copies = []
    for i, piece in enumerate(pieces):
        pc = core if i < 4 else 1 - core
        left, far = i % 4 in (0, 2), i % 4 >= 2
        for near in range(2):
            dx, dy = (near, far) if left else (far, near)
            px = 1 - x if dx else x
            py = 1 - y if dy else y
            for low in range(2):
                for high in range(2):
                    pz = z if low == 0 else z + 1 - 2 * (z % 2)
                    pz = pz if high == 0 else (pz + 2) % 4
                    for start, size, out, place in cuts[0 if left else 1]:
                        source = piece.at[near, low, high, :, pl.ds(start, size)]
                        target = out_refs[out].at[px, pc, pz, py]
                        target = target.at[place] if out else target.at[:, pl.ds(place, size)]
                        copies.append((source, target))
    copies = [pltpu.make_async_copy(*ends, sems.at[i]) for i, ends in enumerate(copies)]
    for copy in copies:
        copy.start()
    for copy in copies:
        copy.wait()


def all_rows(own, other, columns, blocks, split, width, mark):
    rows = own[0].shape[-2]
    cuts = ([], [])
    for low, high, side in ((0, split, 0), (split, columns + blocks * width, 1)):
        start, end = low, min(high, columns)
        if end > start:
            cuts[side].append((start - low, end - start, 0, start))
        for block in range(blocks):
            if low <= columns + block * width < high:
                cuts[side].append((columns + block * width - low, width, 1, block))
    shapes = [jax.ShapeDtypeStruct((2, 2, 4, 2, rows, columns), own[0].dtype)]
    if blocks:
        shapes.append(jax.ShapeDtypeStruct((2, 2, 4, 2, blocks, rows, width), own[0].dtype))
    full = pl.pallas_call(
        functools.partial(place_kernel, cuts),
        in_specs=[pl.BlockSpec(memory_space=pl.ANY if FLAGS["any"] & mark else pltpu.HBM)] * 8,
        out_specs=[pl.BlockSpec(memory_space=pltpu.VMEM)] * len(shapes),
        out_shape=shapes,
        scratch_shapes=[pltpu.SemaphoreType.DMA((32 * (len(cuts[0]) + len(cuts[1])),))],
        compiler_params=pltpu.CompilerParams(vmem_limit_bytes=32 * 1024 * 1024),
        cost_estimate=pl.CostEstimate(
            flops=0, bytes_accessed=128 * rows * (columns + blocks * width), transcendentals=0
        ),
        name="place",
    )(*own, *other)
    return [full[0].reshape(32 * rows, columns)] + [part.reshape(32 * blocks * rows, width) for part in full[1:]]


def pick(array, index, axis):
    return lax.dynamic_index_in_dim(array, index, axis, keepdims=False)


def add_low(left, right):
    return (left.astype(jnp.float32) + right.astype(jnp.float32)).astype(jnp.bfloat16)


def core_rows(left, other):
    _, core, _, _ = grid_place()
    step = left.shape[1] // 4
    first, second, third, fourth = [left[:, i * step : (i + 1) * step] for i in range(4)]
    low = core == (1 if other else 0)
    return jnp.concatenate([jnp.where(low, first, second), jnp.where(low, third, fourth)], axis=1)


def fold_part(part):
    _, core, _, _ = grid_place()
    part = part.reshape(2, 2, 4, 2, -1, part.shape[-1])
    return add_low(pick(part, core, 1), swap_seq(pick(part, 1 - core, 1), CORE_SWAP))


def fold_send(left, right):
    return swap_seq(matmul_left_t(core_rows(left, True), right).astype(jnp.bfloat16), CORE_SWAP)


def fold_core(left, right, got):
    held = (matmul_left_t(core_rows(left, False), right) + got.astype(jnp.float32)).astype(jnp.bfloat16)
    return held.reshape(2, 4, 2, -1, held.shape[-1])


def fold_x(held):
    x, _, _, _ = grid_place()
    return add_low(pick(held, x, 0), swap_seq(pick(held, 1 - x, 0), X_SWAP))


def fold_y(held):
    _, _, _, y = grid_place()
    axis = held.ndim - 3
    return add_low(pick(held, y, axis), swap_ctx(pick(held, 1 - y, axis), Y_SWAP))


def fold_start(left, right):
    return fold_x(left), fold_y(right)


def fold_end(left, right):
    return jnp.concatenate([fold_y(left), fold_x(right)], axis=-1)


def halves(held):
    half = held.shape[-1] // 2
    return held[..., :half], held[..., half:]


def fold_z(line):
    _, _, z, _ = grid_place()
    total = pick(line, z, 0).astype(jnp.float32)
    for k in range(1, 4):
        total = total + swap_ctx(pick(line, (z + k) % 4, 0), Z_SHIFT[k]).astype(jnp.float32)
    return total


def fold_near_z(line):
    _, _, z, _ = grid_place()
    pairs = line.reshape((2, 2) + line.shape[1:])
    return add_low(pick(pairs, z % 2, 1), swap_ctx(pick(pairs, 1 - z % 2, 1), Z_SWAP))


def fold_far_z(held):
    _, _, z, _ = grid_place()
    got = swap_ctx(pick(held, 1 - z // 2, 0), Z_FAR)
    return pick(held, z // 2, 0).astype(jnp.float32) + got.astype(jnp.float32)


def norm_parts(rows):
    width = rows.shape[-1]
    totals = jnp.sum(rows, axis=-1, keepdims=True)
    meansq = (jnp.sum(rows * rows, axis=-1, keepdims=True) + totals * totals) / width
    scale = lax.rsqrt(meansq + EPS)
    last = lax.broadcasted_iota(jnp.int32, rows.shape, 1) == width - 1
    return jnp.where(last, -totals, rows) * scale, scale


def norm_back(normed, scale, gains, grads):
    width = normed.shape[-1]
    weighted = grads * gains
    mean = jnp.sum(weighted * normed, axis=-1, keepdims=True) / width
    grad_u = scale * (weighted - normed * mean)
    last = lax.broadcasted_iota(jnp.int32, grad_u.shape, 1) == width - 1
    final = jnp.sum(jnp.where(last, grad_u, 0.0), axis=-1, keepdims=True)
    return jnp.where(last, 0.0, grad_u - final)


def stack_heads(block):
    head = lax.broadcasted_iota(jnp.int32, block.shape, 1) // HEAD_DIM
    return jnp.concatenate([jnp.where(head == i, block, jnp.zeros_like(block)) for i in range(4)], axis=0)


def unstack_heads(turned):
    rows = turned.T
    head = lax.broadcasted_iota(jnp.int32, (LOCAL, 4 * HEAD_DIM), 1) // HEAD_DIM
    picked = rows[:LOCAL]
    for i in range(1, 4):
        picked = jnp.where(head == i, rows[i * LOCAL : (i + 1) * LOCAL], picked)
    return picked


def attend_kernel(starts, q_ref, k_ref, v_ref, key_ref, query_ref, out_ref, probs_ref, bias_ref):
    window = pl.ds(pl.multiple_of(starts[pl.program_id(0)], 32), WINDOW)

    @pl.when(pl.program_id(1) == 0)
    def _():
        same = key_ref[window, 0:1] == query_ref[0, 0:1, :]
        causal = key_ref[window, 1:2] <= query_ref[0, 1:2, :]
        bias_ref[...] = jnp.where(same & causal, 0.0, NEG)

    stacked = stack_heads(q_ref[...])
    scores = matmul_right_t(k_ref[window, :], stacked) + bias_ref[...]
    weights = jnp.exp(scores - jnp.max(scores, axis=0, keepdims=True))
    probs = (weights * (1.0 / jnp.sum(weights, axis=0, keepdims=True))).astype(jnp.bfloat16)
    probs_ref[0, 0] = probs
    out_ref[...] = unstack_heads(matmul(v_ref[window, :].T, probs)).astype(jnp.bfloat16)


def attend(queries, keys, values, starts, key_marks, query_marks):
    return pl.pallas_call(
        attend_kernel,
        grid_spec=pltpu.PrefetchScalarGridSpec(
            num_scalar_prefetch=1,
            grid=(3, 3),
            in_specs=[
                pl.BlockSpec((LOCAL, 256), lambda j, h, s: (j, h)),
                pl.BlockSpec((KEYS, 256), lambda j, h, s: (0, h)),
                pl.BlockSpec((KEYS, 256), lambda j, h, s: (0, h)),
                pl.BlockSpec((KEYS, 2), lambda j, h, s: (0, 0)),
                pl.BlockSpec((1, 2, 4 * LOCAL), lambda j, h, s: (j, 0, 0)),
            ],
            out_specs=[
                pl.BlockSpec((LOCAL, 256), lambda j, h, s: (j, h)),
                pl.BlockSpec((1, 1, WINDOW, 4 * LOCAL), lambda j, h, s: (j, h, 0, 0)),
            ],
            scratch_shapes=[pltpu.VMEM((WINDOW, 4 * LOCAL), jnp.float32)],
        ),
        out_shape=[
            jax.ShapeDtypeStruct((ROWS, 768), jnp.bfloat16),
            jax.ShapeDtypeStruct((3, 3, WINDOW, 4 * LOCAL), jnp.bfloat16),
        ],
        compiler_params=pltpu.CompilerParams(vmem_limit_bytes=40 * 1024 * 1024),
        cost_estimate=pl.CostEstimate(flops=3_000_000_000, bytes_accessed=12_000_000, transcendentals=2_700_000),
        name="attend",
    )(starts, queries, keys, values, key_marks, query_marks)


def attend_back_kernel(
    starts, q_ref, k_ref, v_ref, grad_ref, probs_ref, grad_q_ref, grad_k_ref, grad_v_ref, sum_k, sum_v
):
    row_block = pl.program_id(1)
    window = pl.ds(pl.multiple_of(starts[row_block], 32), WINDOW)

    @pl.when(row_block == 0)
    def _():
        sum_k[...] = jnp.zeros_like(sum_k)
        sum_v[...] = jnp.zeros_like(sum_v)

    probs = probs_ref[0, 0]
    grads = stack_heads(grad_ref[...])
    wide = probs.astype(jnp.float32)
    terms = wide * matmul_right_t(v_ref[window, :], grads)
    grad_scores = (terms - wide * jnp.sum(terms, axis=0, keepdims=True)).astype(jnp.bfloat16)
    sum_v[window, :] += matmul(probs, grads)
    sum_k[window, :] += matmul(grad_scores, stack_heads(q_ref[...]))
    grad_q = unstack_heads(matmul(k_ref[window, :].T, grad_scores)) * SCALE
    grad_q_ref[...] = grad_q.astype(jnp.bfloat16)

    @pl.when(row_block == 2)
    def _():
        grad_k_ref[...] = sum_k[...].astype(jnp.bfloat16)
        grad_v_ref[...] = sum_v[...].astype(jnp.bfloat16)


def attend_back(queries, keys, values, grads, probs, starts):
    return pl.pallas_call(
        attend_back_kernel,
        grid_spec=pltpu.PrefetchScalarGridSpec(
            num_scalar_prefetch=1,
            grid=(3, 3),
            in_specs=[
                pl.BlockSpec((LOCAL, 256), lambda h, j, s: (j, h)),
                pl.BlockSpec((KEYS, 256), lambda h, j, s: (0, h)),
                pl.BlockSpec((KEYS, 256), lambda h, j, s: (0, h)),
                pl.BlockSpec((LOCAL, 256), lambda h, j, s: (j, h)),
                pl.BlockSpec((1, 1, WINDOW, 4 * LOCAL), lambda h, j, s: (j, h, 0, 0)),
            ],
            out_specs=[
                pl.BlockSpec((LOCAL, 256), lambda h, j, s: (j, h)),
                pl.BlockSpec((KEYS, 256), lambda h, j, s: (0, h)),
                pl.BlockSpec((KEYS, 256), lambda h, j, s: (0, h)),
            ],
            scratch_shapes=[pltpu.VMEM((KEYS, 256), jnp.float32), pltpu.VMEM((KEYS, 256), jnp.float32)],
        ),
        out_shape=[
            jax.ShapeDtypeStruct((ROWS, 768), jnp.bfloat16),
            jax.ShapeDtypeStruct((KEYS, 768), jnp.bfloat16),
            jax.ShapeDtypeStruct((KEYS, 768), jnp.bfloat16),
        ],
        compiler_params=pltpu.CompilerParams(vmem_limit_bytes=40 * 1024 * 1024),
        cost_estimate=pl.CostEstimate(flops=7_000_000_000, bytes_accessed=14_000_000, transcendentals=0),
        name="attend_back",
    )(starts, queries, keys, values, grads, probs)


def widen(array):
    return jnp.pad(array, [(0, 0)] * (array.ndim - 1) + [(0, 1)])


def send_home(delta):
    delta = delta.reshape(3, -1, delta.shape[-1])
    return [swap_ctx(delta[j], RETURN[j]) for j in range(3)]


def at_home(parts, base, ctx):
    home = jnp.zeros((3,) + parts[0].shape, parts[0].dtype)
    for j, part in enumerate(parts):
        home = lax.dynamic_update_index_in_dim(home, part, (2 * j + ctx) % 3, 0)
    return base.astype(jnp.float32) + home[..., : base.shape[-1]].astype(jnp.float32)


def spread_body(
    tokens,
    segment_ids,
    qkv_weight,
    out_weight,
    up_weight,
    down_weight,
    attn_gain,
    mlp_gain,
    out_cotangent,
):
    micro_count, _, local_len, res_width = tokens.shape
    width = res_width + 1
    ctx = lax.axis_index("ctx")
    tokens = tokens.reshape(micro_count, local_len, res_width)
    cotangent = out_cotangent.reshape(micro_count, local_len, res_width)

    gains_own = jnp.pad(jnp.stack([attn_gain, mlp_gain], axis=1), ((0, 0), (0, 126)))
    rows_own, ff = up_weight.shape
    def deal(array):
        return [swap_ctx(pick(array, (2 * j + ctx) % 3, 0), DEAL[j]) for j in range(3)]

    def meet(flag, *values):
        return lax.optimization_barrier(values) if FLAGS[flag] else values

    wide, cotangent_wide = widen(tokens), widen(cotangent)
    if FLAGS["deal"] == 1:
        both = deal(jnp.concatenate([wide, cotangent_wide], axis=1))
        dealt = [part[:local_len] for part in both]
        grad_rows = [part[local_len:] for part in both]
    else:
        dealt, grad_rows = deal(wide), []
    far = swap_ctx(wide[1], [(0, 5)])
    early_own = jnp.concatenate([qkv_weight, gains_own], axis=1)
    early_cut = FLAGS["cut"]
    up_own, down_own = jnp.concatenate([widen(out_weight), up_weight], axis=1), widen(down_weight)
    pair = jnp.stack([early_own, swap_ctx(early_own, Z_FAR)])
    pair, up_own, down_own = meet("f0", pair, up_own, down_own)
    line = jnp.stack([pair, swap_ctx(pair, Z_SWAP)])
    dealt, far, line, up_own, down_own, cotangent_wide, grad_rows = meet(
        "f1", dealt, far, line, up_own, down_own, cotangent_wide, grad_rows
    )
    inputs_low = jnp.concatenate(dealt, axis=0)
    near = plane_start(line, early_cut)
    up_own, line = lax.optimization_barrier((up_own, line))
    up_pair = jnp.stack([up_own, swap_ctx(up_own, Z_FAR)])
    if FLAGS["deal"] == 0:
        grad_rows = [swap_ctx(pick(cotangent_wide, (2 * j + ctx) % 3, 0), DEAL[j]) for j in range(2)]
    near, up_pair, inputs_low = meet("f2", near, up_pair, inputs_low)
    ends = plane_end(*near)
    up_line = jnp.stack([up_pair, swap_ctx(up_pair, Z_SWAP)])
    if FLAGS["deal"] == 0:
        grad_rows.append(swap_ctx(pick(cotangent_wide, (4 + ctx) % 3, 0), DEAL[2]))
    up_line, ends, inputs_low, grad_rows = meet("f3", up_line, ends, inputs_low, grad_rows)
    pieces = [*near, *ends]
    others = other_core(pieces)
    up_near = plane_start(up_line, (width + ff) // 2)
    down_own, up_line = lax.optimization_barrier((down_own, up_line))
    if FLAGS["deal"] == 5:
        cotangent_wide, up_near = lax.optimization_barrier((cotangent_wide, up_near))
    down_pair = jnp.stack([down_own, swap_ctx(down_own, Z_FAR)])
    below = [None, None]
    if FLAGS["shift"] in (0, 1):
        below[0] = swap_ctx(inputs_low, UP[0])
    if FLAGS["shift"] == 0:
        below[1] = swap_ctx(inputs_low, UP[1])
    up_near, down_pair, others, below, inputs_low, cotangent_wide = meet(
        "f4", up_near, down_pair, others, below, inputs_low, cotangent_wide
    )
    (first,) = all_rows(pieces, others, early_own.shape[1], 0, early_cut, width, 1)
    up_ends = plane_end(*up_near)
    down_line = jnp.stack([down_pair, swap_ctx(down_pair, Z_SWAP)])
    if FLAGS["deal"] == 6:
        cotangent_wide, up_ends = lax.optimization_barrier((cotangent_wide, up_ends))
    if FLAGS["shift"] == 2:
        below[0] = swap_ctx(inputs_low, UP[0])
    if FLAGS["shift"] in (1, 2):
        below[1] = swap_ctx(inputs_low, UP[1])
    down_line, up_ends, below, _ = meet("f5", down_line, up_ends, below, first)
    if FLAGS["deal"] == 4:
        cotangent_wide, down_line = lax.optimization_barrier((cotangent_wide, down_line))
    if FLAGS["deal"] in (3, 4, 5, 6):
        grad_rows = deal(cotangent_wide)
    down_near = plane_start(down_line, width // 2)
    up_others = other_core([*up_near, *up_ends])
    key_rows = jnp.concatenate([far, below[1], below[0], inputs_low], axis=0).astype(jnp.float32)
    q_full, second = first[:, :width], first[:, width : 3 * width]
    gain_one = first[:, 3 * width].astype(jnp.float32)
    gain_two = first[:, 3 * width + 1].astype(jnp.float32)

    ids = segment_ids.reshape(micro_count, -1) + 8 * jnp.arange(micro_count, dtype=jnp.int32)[:, None]
    ids = jnp.concatenate([jnp.full((KEYS - ROWS,), -1, jnp.int32), ids.reshape(-1)])
    ids = lax.dynamic_slice_in_dim(ids, ROWS * ctx, KEYS, 0)
    places = jnp.arange(KEYS, dtype=jnp.int32)
    key_marks = jnp.stack([ids, places], axis=1)
    query_marks = jnp.stack([ids, places])[:, KEYS - ROWS :].reshape(2, 3, local_len)
    query_marks = jnp.tile(jnp.moveaxis(query_marks, 0, 1), (1, 1, 4))
    flat = 3 * ctx + jnp.arange(3, dtype=jnp.int32)
    starts = jnp.clip(8 * (flat // 8) + 7 - 3 * ctx, 0, 2) * local_len

    inputs = key_rows[KEYS - ROWS :]
    key_normed, key_scale = norm_parts(key_rows)
    norm_keys = (key_normed * gain_one).astype(jnp.bfloat16)
    norm_a = norm_keys[KEYS - ROWS :]
    if FLAGS["kvg"]:
        norm_keys, norm_a, down_near = lax.optimization_barrier((norm_keys, norm_a, down_near))
    queries = (matmul(norm_a, q_full).astype(jnp.bfloat16) * SCALE).astype(jnp.bfloat16)
    keys_values = matmul(norm_keys, second).astype(jnp.bfloat16)
    keys, values = keys_values[:, :width], keys_values[:, width:]
    queries, keys, values, down_near, up_others = meet("f6", queries, keys, values, down_near, up_others)
    down_ends = plane_end(*down_near)
    down_others = other_core(down_near)
    if FLAGS["deal"] == 2:
        grad_rows = deal(cotangent_wide)
    attn, probs = attend(queries, keys, values, starts, key_marks, query_marks)
    attn, down_ends, up_others, down_others, grad_rows = meet("f7", attn, down_ends, up_others, down_others, grad_rows)
    grad_rows = jnp.concatenate(grad_rows, axis=0)
    down_pieces = [*down_near, *down_ends]
    down_others = down_others + other_core(down_ends)
    (out_up_full,) = all_rows([*up_near, *up_ends], up_others, width + ff, 0, (width + ff) // 2, width, 2)
    out_full, up_full = out_up_full[:, :width], out_up_full[:, width:]
    branch = matmul(attn, out_full)
    mixed = inputs + branch
    mixed_normed, mixed_scale = norm_parts(mixed)
    norm_m = (mixed_normed * gain_two).astype(jnp.bfloat16)
    if FLAGS["f8"] == 1:
        norm_m, down_others = meet("f8", norm_m, down_others)
    pre = matmul(norm_m, up_full)
    if FLAGS["f8"] == 2:
        pre, down_others = meet("f8", pre, down_others)
    (down_full,) = all_rows(down_pieces, down_others, width, 0, width // 2, width, 4)
    act, gelu_pull = jax.vjp(gelu_tanh, pre)
    act = act.astype(jnp.bfloat16)

    if FLAGS["dfold"]:
        down_got = fold_send(act, grad_rows)
    else:
        grad_down = matmul_left_t(act, grad_rows).astype(jnp.bfloat16)
        grad_rows, grad_down = lax.optimization_barrier((grad_rows, grad_down))
        down_got = fold_part(grad_down)
    grad_pre = gelu_pull(matmul_right_t(grad_rows, down_full))[0].astype(jnp.bfloat16)
    if not FLAGS["late_result"]:
        result_delta = (branch + matmul(act, down_full)).astype(jnp.bfloat16)
    home, deltas = [], []
    down_got, grad_pre = meet("b0", down_got, grad_pre)
    down_near = fold_start(*halves(fold_core(act, grad_rows, down_got) if FLAGS["dfold"] else down_got))
    if FLAGS["ufold"]:
        up_got = fold_send(norm_m, grad_pre)
    else:
        grad_up = matmul_left_t(norm_m, grad_pre).astype(jnp.bfloat16)
        up_held = fold_part(grad_up)
        if FLAGS["upfirst"]:
            grad_pre, grad_up = lax.optimization_barrier((grad_pre, grad_up))
    grad_norm_m = matmul_right_t(grad_pre, up_full)
    grad_gain_two = jnp.sum(grad_norm_m * mixed_normed, axis=0)
    grad_mixed_norm = norm_back(mixed_normed, mixed_scale, gain_two, grad_norm_m)
    grad_branch = (grad_rows.astype(jnp.float32) + grad_mixed_norm).astype(jnp.bfloat16)
    grad_attn = matmul_right_t(grad_branch, out_full).astype(jnp.bfloat16)
    if FLAGS["ufold"]:
        up_held = fold_core(norm_m, grad_pre, up_got)
    if FLAGS["outin"]:
        grad_out = matmul_left_t(attn, grad_branch).astype(jnp.bfloat16)
        grad_attn, grad_out = meet("b1", grad_attn, grad_out)
    grad_attn, grad_branch, down_near, up_held, home, deltas = meet(
        "b2", grad_attn, grad_branch, down_near, up_held, home, deltas
    )
    down_line, up_near = fold_end(*down_near), fold_start(*halves(up_held))
    grad_q, grad_k, grad_v = attend_back(queries, keys, values, grad_attn, probs, starts)
    grad_q, grad_k, grad_v, down_line, up_near, act = meet("b3", grad_q, grad_k, grad_v, down_line, up_near, act)
    up_line = fold_end(*up_near)
    down_pair = fold_near_z(down_line)
    grad_kv = jnp.concatenate([grad_k, grad_v], axis=1)
    grad_norm_keys = matmul_right_t(grad_kv, second)
    grad_below = grad_norm_keys[: KEYS - ROWS].astype(jnp.bfloat16)
    if FLAGS["dxfirst"]:
        grad_kv, grad_q, grad_below = lax.optimization_barrier((grad_kv, grad_q, grad_below))
    sent = [grad_below[4 * local_len :], grad_below[local_len : 4 * local_len], grad_below[:local_len]]
    swaps = [[(high, low) for low, high in pairs] for pairs in UP]
    back = [swap_ctx(sent[i], swaps[i]) for i in range(2)]
    if FLAGS["u2"] == 1:
        grad_kv, grad_q, up_line, down_pair = lax.optimization_barrier((grad_kv, grad_q, up_line, down_pair))
    grad_norm_q = matmul_right_t(grad_q, q_full)
    grad_gain_one = jnp.sum(grad_norm_keys * key_normed, axis=0)
    grad_gain_one = grad_gain_one + jnp.sum(grad_norm_q * key_normed[KEYS - ROWS :], axis=0)
    gains = jnp.pad(jnp.stack([grad_gain_one, grad_gain_two], axis=1).astype(jnp.bfloat16), ((0, 0), (0, 126)))
    _, core, _, _ = grid_place()
    grad_q_weight = matmul_left_t(norm_a, grad_q).astype(jnp.bfloat16)
    grad_kv_weight = matmul_left_t(norm_keys, grad_kv).astype(jnp.bfloat16)
    early_parts = [part.reshape(2, 2, 8 * rows_own, -1) for part in (grad_q_weight, grad_kv_weight, grad_out, gains)]
    early_sent = jnp.concatenate([pick(part, 1 - core, 1) for part in early_parts], axis=-1)
    if FLAGS["u2"] == 2:
        early_sent, up_line, down_pair = lax.optimization_barrier((early_sent, up_line, down_pair))
    if FLAGS["dfar"]:
        grad_down = fold_far_z(down_pair)
    if FLAGS["ab"] == 1:
        early_sent, back = meet("ab", early_sent, back)
    early_got = swap_seq(early_sent, CORE_SWAP)
    early_held = add_low(jnp.concatenate([pick(part, core, 1) for part in early_parts], axis=-1), early_got)
    if FLAGS["dfar"]:
        if FLAGS["b4"] == 1:
            early_held, up_line, grad_down, back = meet("b4", early_held, up_line, grad_down, back)
        else:
            early_held, up_line = meet("b4", early_held, up_line)
    elif FLAGS["b4"] == 1:
        early_held, up_line, down_pair, back = meet("b4", early_held, up_line, down_pair, back)
    else:
        early_held, up_line, down_pair = meet("b4", early_held, up_line, down_pair)
    if FLAGS["late_result"]:
        early_held, act = lax.optimization_barrier((early_held, act))
        result_delta = (branch + matmul(act, down_full)).astype(jnp.bfloat16)
    deltas = result_delta.reshape(3, local_len, width)
    early_held = early_held.reshape(2, 4, 2, rows_own, -1)
    early_near = fold_start(early_held[..., : 2 * width], early_held[..., 2 * width :])
    last = sent[2]
    if FLAGS["b4"] == 3:
        early_near, back, last = meet("b4", early_near, back, last)
    elif FLAGS["c"]:
        back, last = meet("c", back, last)
    back = back + [swap_ctx(last, swaps[2])]
    if FLAGS["b6"] == 2:
        early_near, up_line, down_pair = meet("b6", early_near, up_line, down_pair)
    if not FLAGS["dfar"]:
        grad_down = fold_far_z(down_pair)
    up_pair = fold_near_z(up_line)
    if FLAGS["b6"] == 1:
        early_near, up_pair, grad_down, back = meet("b6", early_near, up_pair, grad_down, back)
    early_line = fold_end(*early_near)
    grad_norm_a = grad_norm_keys[KEYS - ROWS :] + grad_norm_q + back[0].astype(jnp.float32) + back[1].astype(jnp.float32)
    grad_norm_a = grad_norm_a + jnp.pad(back[2].astype(jnp.float32), ((2 * local_len, 0), (0, 0)))
    grad_input_norm = norm_back(
        key_normed[KEYS - ROWS :], key_scale[KEYS - ROWS :], gain_one, grad_norm_a
    )
    grad_delta = (grad_mixed_norm + grad_input_norm).astype(jnp.bfloat16)
    if FLAGS["lz"] == 1:
        early_line, up_pair = meet("lz", early_line, up_pair)
    late_sum = fold_far_z(up_pair)
    deltas = jnp.stack([deltas, grad_delta.reshape(3, local_len, width)], axis=1)
    if FLAGS["homeg"] == 1:
        deltas, early_line = meet("homeg", deltas, early_line)
    early_pair = fold_near_z(early_line)
    if FLAGS["homeg"] == 2:
        deltas, early_pair = meet("homeg", deltas, early_pair)
    parts = send_home(deltas)
    if FLAGS["b7"]:
        early_pair, late_sum = meet("b7", early_pair, late_sum)
    early_sum = fold_far_z(early_pair)
    if FLAGS["homeg"] == 3:
        early_sum, parts = meet("homeg", early_sum, parts)
    result = at_home([part[:local_len] for part in parts], tokens, ctx)
    grad_tokens = at_home([part[local_len:] for part in parts], cotangent, ctx)
    grad_up = late_sum
    grad_qkv, grad_out = early_sum[:, : 3 * width], early_sum[:, 3 * width : 4 * width]
    grad_gain_one, grad_gain_two = early_sum[:, 4 * width], early_sum[:, 4 * width + 1]
    shape = (micro_count, 1, local_len, res_width)
    return (
        result.reshape(shape),
        grad_tokens.reshape(shape),
        grad_qkv,
        grad_out[:, :res_width],
        grad_up,
        grad_down[:, :res_width],
        grad_gain_one,
        grad_gain_two,
    )


def solution(mesh):
    small = (mesh.shape["seq"], mesh.shape["ctx"]) == (4, 8)
    return jax.shard_map(
        spread_body if small else body,
        mesh=mesh,
        in_specs=(
            P(None, "seq", "ctx", None),
            P(None, "seq", None),
            P(("seq", "ctx"), None),
            P(("seq", "ctx"), None),
            P(("seq", "ctx"), None),
            P(("seq", "ctx"), None),
            P(("seq", "ctx")),
            P(("seq", "ctx")),
            P(None, "seq", "ctx", None),
        ),
        out_specs=(
            P(None, "seq", "ctx", None),
            P(None, "seq", "ctx", None),
            P(("seq", "ctx"), None),
            P(("seq", "ctx"), None),
            P(("seq", "ctx"), None),
            P(("seq", "ctx"), None),
            P(("seq", "ctx")),
            P(("seq", "ctx")),
        ),
        check_vma=False,
    )
```
